256 devices in a mesh: slab: 64 (over x, z, core), sub: 4 (over y).
Axes of the slice: x: 4, y: 4, z: 8, core: 2. Of those that a mesh axis runs over, the one named last changes fastest.
Arguments:
- charge_grid: float32 [512, 256, 512], P('slab', 'sub'), may hold values from -6 to 6
- atom_offset: float32 [3, 4194304], P(None, ('slab', 'sub')), may hold values from 0 to 8
- block_cell: int32 [32768], P(('slab', 'sub')), may hold values from 0 to 511
- block_count: int32 [32768], P(('slab', 'sub')), may hold values from 0 to 128, as said below
Outputs:
- atom_field: float32 [4, 4194304], P(None, ('slab', 'sub'))
The draws below stay inside these ranges and needn't reach their ends.
Inputs may be any that keep to these rules, and one draw needn't show every extreme that they name: `block_count`: on each device the blocks that hold atoms come first, and its first block holds 128 atoms; a block's atoms fill its lowest slots. Some device has atoms in all 128 blocks and some in only 32.
All inputs are finite; a program needn't handle non-finite values.
Results may differ from the reference program's by a relative error of at most 0.0003.
Values sent between devices are 32-bit elements; how exact they have to be, the bound alone decides.
No kernel may reach another device: no remote copies, remote signals or barrier semaphores. Data moves between devices by JAX's collectives and lax.ppermute only.
A program may use at most 128 MiB of HBM per device.

```python
import math
import jax
import jax.numpy as jnp
from jax import lax

CZ = 8
CY = 64
NX = 512
NBLK = 128
SLOT = 128
BRICK = 8
NZ = 512
NY = 256
BLOCKS = 32768
ATOMS = 4194304
BRICKS = 512
N_SLAB = 64
N_SUB = 4


def draw_block_count(key, part):
    device_total = BLOCKS // NBLK
    first_key = jax.random.fold_in(key, 11)
    second_key = jax.random.fold_in(key, 12)
    third_key = jax.random.fold_in(key, 13)
    fourth_key = jax.random.fold_in(key, 14)
    live = jax.random.randint(first_key, (device_total,), NBLK // 4, NBLK + 1)
    full_device = jax.random.randint(third_key, (), 0, device_total)
    low_device = (full_device + 1 + jax.random.randint(fourth_key, (), 0, device_total - 1)) % device_total
    device_index = jnp.arange(device_total)
    live = jnp.where(device_index == full_device, NBLK, live)
    live = jnp.where(device_index == low_device, NBLK // 4, live)
    counts = jax.random.randint(second_key, (device_total, NBLK), 48, SLOT + 1)
    slot_index = jnp.arange(NBLK)
    counts = jnp.where(slot_index[None, :] == 0, SLOT, counts)
    counts = jnp.where(slot_index[None, :] < live[:, None], counts, 0)
    return counts.reshape(BLOCKS).astype(jnp.int32)


def plant(entries, key, low, top_value):
    extent = entries.shape
    place = [jax.random.randint(jax.random.fold_in(key, axis), (), 0, extent[axis]) for axis in range(len(extent))]
    entries = entries.at[tuple(place)].set(low)
    longest = extent.index(max(extent))
    place[longest] = (place[longest] + 1) % extent[longest]
    return entries.at[tuple(place)].set(top_value)


def block_scale(own_key, dims, cuts, low, top_value):
    gain, own = 1.0, jax.random.fold_in(own_key, 6)
    for axis_at, blocks in cuts:
        heights = jnp.exp(jax.random.uniform(jax.random.fold_in(own, axis_at), (blocks,), jnp.float32, low / len(cuts), top_value / len(cuts)))
        gain = gain * jnp.repeat(heights, dims[axis_at] // blocks).reshape([-1 if axis == axis_at else 1 for axis in range(len(dims))])
    return gain


def bell_draw(stream_key, dims, scale, bound, cuts=(), kind=jnp.bfloat16):
    values = jax.random.normal(stream_key, dims, jnp.float32) * scale
    if len(cuts) > 0:
        values = block_scale(stream_key, dims, cuts, -0.22, 0.18) * values
    return jnp.clip(values, min=-bound, max=bound).astype(kind)


def setup_inputs(seed: int = 0) -> dict:
    arg_keys = jax.random.split(jax.random.key(seed), 5)
    charge_grid = bell_draw(arg_keys[0], (NZ, NY, NX), 1.0, 6.0, ((0, 64), (1, 4)), jnp.float32)
    atom_offset = jnp.clip(8.0 * jax.random.uniform(arg_keys[1], (3, ATOMS), jnp.float32) ** block_scale(arg_keys[1], (3, ATOMS), ((1, 256),), -0.2, 0.2), 0.0, 8.0)
    block_cell = plant(jax.random.randint(arg_keys[2], (BLOCKS,), 0, BRICKS), jax.random.fold_in(arg_keys[2], 1), 0, BRICKS - 1).astype(jnp.int32)
    block_count = draw_block_count(jax.random.fold_in(arg_keys[4], 71), 0)
    return dict(charge_grid=charge_grid, atom_offset=atom_offset, block_cell=block_cell, block_count=block_count)


TAPS = (0.125, 0.5, 0.75, 0.5, 0.125)
SPANS = (2.0, 8.0, 32.0)
NEAR_WEIGHT = 0.5
HIGH = lax.Precision.HIGHEST


def pad_along(values, axis, width):
    widths = [(0, 0)] * values.ndim
    widths[axis] = (width, width)
    return jnp.pad(values, widths)


def restrict_axis(values, axis, halo_width, margin, coarse_own):
    length = 2 * (coarse_own + 2 * margin - 1) + 1
    total = None
    for offset in range(5):
        start = halo_width - 2 * margin + offset - 2
        term = TAPS[offset] * lax.slice_in_dim(values, start, start + length, 2, axis)
        total = term if total is None else total + term
    return total


def prolong_axis(values, axis, halo_width, margin, coarse_own):
    base = halo_width - margin // 2
    count = coarse_own + margin

    def take(start):
        return lax.slice_in_dim(values, start, start + count, 1, axis)

    even = 0.125 * take(base - 1) + 0.75 * take(base) + 0.125 * take(base + 1)
    odd = 0.5 * take(base) + 0.5 * take(base + 1)
    joined = jnp.stack([even, odd], axis=axis + 1)
    shape = list(even.shape)
    shape[axis] = 2 * count
    return joined.reshape(shape)


def smooth_axis(values, axis, halo_width, margin, own):
    total = None
    for offset in range(5):
        weight = math.exp(-0.5 * (offset - 2) ** 2)
        start = halo_width - margin + offset - 2
        term = weight * lax.slice_in_dim(values, start, start + own + 2 * margin, 1, axis)
        total = term if total is None else total + term
    return total


def gauss_rows(row_index, count, span):
    diff = row_index.astype(jnp.float32)[:, None] - jnp.arange(count).astype(jnp.float32)[None, :]
    return jnp.exp(-(diff / span) ** 2)


def spline(shifted):
    at = jnp.abs(shifted)
    inner = 2.0 / 3.0 - at * at + 0.5 * at * at * at
    outer = jnp.maximum(2.0 - at, 0.0)
    return jnp.where(at < 1.0, inner, outer * outer * outer / 6.0)


def spline_slope(shifted):
    at = jnp.abs(shifted)
    inner = -2.0 * shifted + 1.5 * shifted * at
    outer = jnp.maximum(2.0 - at, 0.0)
    return jnp.where(at < 1.0, inner, -0.5 * outer * outer * jnp.sign(shifted))


def interpolate(patches, offsets, counts):
    grid_index = jnp.arange(patches.shape[1]).astype(offsets.dtype)
    shifted = offsets[:, :, None, :] + 2.0 - grid_index[None, None, :, None]
    weights = spline(shifted)
    slopes = spline_slope(shifted)
    paired = jnp.stack([weights[2], slopes[2]], axis=2)
    inner = jnp.einsum("gkji,gica->gkjca", patches, paired, precision=HIGH)
    base = inner[:, :, :, 0]
    along_x = inner[:, :, :, 1]
    value = jnp.einsum("gkja,gka,gja->ga", base, weights[0], weights[1], precision=HIGH)
    field_z = -jnp.einsum("gkja,gka,gja->ga", base, slopes[0], weights[1], precision=HIGH)
    field_y = -jnp.einsum("gkja,gka,gja->ga", base, weights[0], slopes[1], precision=HIGH)
    field_x = -jnp.einsum("gkja,gka,gja->ga", along_x, weights[0], weights[1], precision=HIGH)
    live = (jnp.arange(offsets.shape[2], dtype=jnp.int32)[None, :] < counts[:, None]).astype(offsets.dtype)
    return jnp.stack([value, field_z, field_y, field_x]) * live[None]


def restrict_all(values):
    for axis in range(3):
        values = restrict_axis(pad_along(values, axis, 2), axis, 2, 0, values.shape[axis] // 2)
    return values


def prolong_all(values):
    for axis in range(3):
        values = prolong_axis(pad_along(values, axis, 1), axis, 1, 0, values.shape[axis])
    return values


def smooth_all(values):
    for axis in range(3):
        values = smooth_axis(pad_along(values, axis, 2), axis, 2, 0, values.shape[axis])
    return values


def top_apply(top):
    result = jnp.zeros(top.shape, jnp.float32)
    for span in SPANS:
        kernel_z = span ** -1.5 * gauss_rows(jnp.arange(top.shape[0]), top.shape[0], span)
        kernel_y = gauss_rows(jnp.arange(top.shape[1]), top.shape[1], span)
        kernel_x = gauss_rows(jnp.arange(top.shape[2]), top.shape[2], span)
        mixed = jnp.einsum("ai,ijk->ajk", kernel_z, top, precision=HIGH)
        mixed = jnp.einsum("bj,ajk->abk", kernel_y, mixed, precision=HIGH)
        result = result + jnp.einsum("ck,abk->abc", kernel_x, mixed, precision=HIGH)
    return result


def reference(charge_grid, atom_offset, block_cell, block_count):
    coarse = restrict_all(charge_grid)
    top = restrict_all(coarse)
    top_potential = top_apply(top)
    middle = prolong_all(top_potential)
    near = smooth_all(charge_grid)
    fine = prolong_all(middle) + NEAR_WEIGHT * near
    padded = jnp.pad(fine, 2)
    devices = N_SLAB * N_SUB
    offsets = atom_offset.reshape(3, devices, NBLK, SLOT).transpose(1, 0, 2, 3)
    cells = block_cell.reshape(devices, NBLK)
    counts = block_count.reshape(devices, NBLK)
    bricks_y = CY // BRICK
    bricks_x = NX // BRICK
    patch_size = BRICK + 4

    def one_device(items):
        device, offset_part, cell_part, count_part = items
        z_start = CZ * (device // N_SUB) + BRICK * (cell_part // (bricks_y * bricks_x))
        y_start = CY * (device % N_SUB) + BRICK * ((cell_part // bricks_x) % bricks_y)
        x_start = BRICK * (cell_part % bricks_x)

        def cut(first, second, third):
            return lax.dynamic_slice(padded, (first, second, third), (patch_size, patch_size, patch_size))

        patches = jax.vmap(cut)(z_start.astype(jnp.int32), y_start.astype(jnp.int32), x_start.astype(jnp.int32))
        return interpolate(patches, offset_part, count_part)

    fields = lax.map(one_device, (jnp.arange(devices, dtype=jnp.int32), offsets, cells, counts))
    return fields.transpose(1, 0, 2, 3).reshape(4, devices * NBLK * SLOT)
```

```python
import math

import jax
import jax.numpy as jnp
import ml_dtypes
import numpy as np
from jax import lax
from jax.experimental import pallas as pl
from jax.experimental.pallas import tpu as pltpu
from jax.sharding import PartitionSpec as P

TAPS = (0.125, 0.5, 0.75, 0.5, 0.125)
SPANS = (2.0, 8.0, 32.0)
NEAR_WEIGHT = 0.5

SLABS, SUBS = 64, 4
CZ, CY, NX = 8, 64, 512
NZ, NY = CZ * SLABS, CY * SUBS
BLOCKS, SLOT = 128, 128

FZ, FY, FX = 16, 72, 640
TZ, TY, TYS = 5, 19, 24
GS = 21
TILE = 40
TILES = 16

F32, BF16 = jnp.float32, jnp.bfloat16


def restriction(n):
    matrix = np.zeros((n // 2, n))
    for target in range(n // 2):
        for offset in range(-2, 3):
            if 0 <= 2 * target + offset < n:
                matrix[target, 2 * target + offset] = TAPS[offset + 2]
    return matrix


def restriction_twice(n):
    return restriction(n // 2) @ restriction(n)


def gauss(n, span):
    index = np.arange(n, dtype=np.float64)
    return np.exp(-(((index[:, None] - index[None, :]) / span) ** 2))


def window(matrix, row0, rows, col0, cols):
    out = np.zeros((rows, cols))
    for r in range(rows):
        for c in range(cols):
            if 0 <= row0 + r < matrix.shape[0] and 0 <= col0 + c < matrix.shape[1]:
                out[r, c] = matrix[row0 + r, col0 + c]
    return out


def halves(matrix):
    whole = np.asarray(matrix, np.float32)
    high = whole.astype(ml_dtypes.bfloat16)
    low = (whole - high.astype(np.float32)).astype(ml_dtypes.bfloat16)
    return high, low


def split(values):
    high = values.astype(BF16)
    return high, (values - high.astype(F32)).astype(BF16)


def dot(left, right):
    return jnp.dot(left, right, preferred_element_type=F32)


def dot3(left_high, left_low, right_high, right_low):
    return dot(left_high, right_high) + (dot(left_low, right_high) + dot(left_high, right_low))


SLAB_KINDS = (0, 1, SLABS - 1)


def make_constants():
    rz, ry, rx = restriction_twice(NZ), restriction_twice(NY), restriction_twice(NX)
    restrict_x = rx.T.astype(ml_dtypes.bfloat16)
    restrict_zy = np.zeros((3, SUBS, CZ, CY, 128))
    for kind, p in enumerate(SLAB_KINDS):
        mz = window(rz, 2 * p - 1, TZ, CZ * p, CZ)
        for q in range(SUBS):
            my = window(ry, 16 * q - 1, TY, CY * q, CY)
            for zt in range(TZ):
                restrict_zy[kind, q, :, :, zt * TYS : zt * TYS + TY] = (
                    mz[zt][:, None, None] * my.T[None, :, :]
                )
    restrict_zy = restrict_zy.reshape(3 * SUBS, CZ * CY, 128).astype(np.float32)

    span_y = np.zeros((SUBS, 128, 3 * 128))
    span_z = np.zeros((TZ, SLABS, 3, 2, SLABS))
    fine_x = np.zeros((SLABS, 8, FX))
    for s, span in enumerate(SPANS):
        gy, gz, gx = gauss(NY // 4, span), gauss(NZ // 4, span), gauss(NX // 4, span)
        for q in range(SUBS):
            part = window(gy, 16 * q - 1, TY, 0, NY // 4).T
            for x in range(2):
                col = s * 128 + (s * 2 + x) * GS
                span_y[q, x * 64 : x * 64 + 64, col : col + TY] = part
        wide = np.zeros((NZ // 4 + 8, NZ // 4))
        wide[1 : 1 + NZ // 4] = gz * span ** (-1.5)
        for k in range(TZ):
            rows = wide[k : k + NZ // 4 : 2]
            span_z[k, :, s] = rows.reshape(SLABS, SLABS, 2).transpose(0, 2, 1)
        px = rx.T @ gx
        for x in range(2):
            fine_x[:, s * 2 + x, 1 : 1 + NX] = px[:, x::2].T
    span_z = span_z.reshape(TZ * SLABS, 3 * 128)
    fine_x = fine_x.reshape(SLABS * 8, FX)

    prolong_y = np.zeros((SUBS, FY, FZ, 128))
    for q in range(SUBS):
        part = window(ry.T, CY * q - 1, CY + 3, 16 * q - 1, TY)
        for zo in range(TZ):
            prolong_y[q, : CY + 3, :, zo * TYS : zo * TYS + TY] = part[:, None, :]
    prolong_y = prolong_y.reshape(SUBS, FY * FZ, 128).astype(ml_dtypes.bfloat16)
    prolong_z = np.zeros((3, 8, FZ, 128))
    for kind, p in enumerate(SLAB_KINDS):
        part = window(rz.T, CZ * p - 1, CZ + 3, 2 * p - 1, TZ)
        for zo in range(TZ):
            prolong_z[kind, :, : CZ + 3, zo * TYS : zo * TYS + TY] = part[None, :, zo, None]
    prolong_z = prolong_z.reshape(3, 8 * FZ, 128).astype(np.float32)
    return dict(
        restrict_x=restrict_x,
        restrict_zy=restrict_zy,
        span_y=halves(span_y),
        span_z=halves(span_z),
        fine_x=halves(fine_x),
        prolong_y=prolong_y,
        prolong_z=prolong_z,
    )


CONSTANTS = make_constants()


def restrict_kernel(place, charge, along_x, along_zy, out):
    values = charge[...].reshape(CZ * CY, NX)
    high, low = split(values)
    narrow = dot(high, along_x[...]) + dot(low, along_x[...])
    narrow_high, narrow_low = split(narrow.T)
    zy_high, zy_low = split(along_zy[0])
    out[...] = dot3(narrow_high, narrow_low, zy_high, zy_low)


def middle_kernel(place, own, one, two, three, y_high, y_low, z_high, z_low, out):
    q = place[1]
    lane = lax.broadcasted_iota(jnp.int32, (SLABS, 128), 1)
    gathered = [None] * TZ
    for back, ref in enumerate((own, one, two, three)):
        source = lax.rem(q + (SUBS - back), SUBS)
        for x in range(2):
            rows = ref[pl.ds(x, SLABS, stride=2), :]
            first = 64 * x - 1 + 16 * source
            inside = (lane >= first) & (lane < first + TY)
            for zt in range(TZ):
                shift = lax.rem(first + (256 - TYS * zt), 128)
                term = jnp.where(inside, pltpu.roll(rows, shift, 1), 0.0)
                gathered[zt] = term if gathered[zt] is None else gathered[zt] + term
    even = gathered[1] + pltpu.roll(gathered[3], 1, 0)
    odd = gathered[2] + pltpu.roll(gathered[4], 1, 0) + pltpu.roll(gathered[0], SLABS - 1, 0)
    top_high, top_low = split(jnp.concatenate([even, odd], axis=0))
    mixed = dot3(top_high, top_low, y_high[0], y_low[0])
    stacked = jnp.concatenate([mixed[:, :128], mixed[:, 128:256], mixed[:, 256:]], axis=0)
    stacked_high, stacked_low = split(stacked)
    folded = dot3(z_high[...], z_low[...], stacked_high, stacked_low)
    for g in range(6):
        total = None
        for k in range(TZ):
            piece = folded[k * SLABS : (k + 1) * SLABS]
            moved = pltpu.roll(piece, (256 + TYS * k - GS * g) % 128, 1)
            term = jnp.where((lane >= TYS * k) & (lane < TYS * k + TY), moved, 0.0)
            total = term if total is None else total + term
        out[pl.ds(g, SLABS, stride=8), :] = total
    for g in range(6, 8):
        out[pl.ds(g, SLABS, stride=8), :] = jnp.zeros((SLABS, 128), F32)


def near_kernel(place, charge, z_low, z_high, y_low, y_high, out, rows, wide):
    p, q = place[0], place[1]
    taps = [math.exp(-0.5 * d * d) for d in range(3)]

    def stencil(at):
        return taps[2] * (at(0) + at(4)) + (taps[1] * (at(1) + at(3)) + at(2))

    def plane(k):
        if k < 3:
            return z_low[k]
        return charge[k - 3] if k < 3 + CZ else z_high[k - 3 - CZ]

    node = lax.broadcasted_iota(jnp.int32, (FY, 128), 0) + (CY * q - 1)
    keep_y = jnp.where((node >= 0) & (node < NY), NEAR_WEIGHT, 0.0)
    keep_y = jnp.concatenate([keep_y] * (NX // 128), axis=1)
    wide[0] = jnp.zeros((FY * FZ, 128), F32)
    wide[1 + NX // 128] = jnp.zeros((FY * FZ, 128), F32)
    for zo in range(CZ + 3):
        rows[8 : 8 + CY] = stencil(lambda d: plane(zo + d))
        rows[4:8] = stencil(lambda d: y_low[zo + d])
        rows[8 + CY : 12 + CY] = stencil(lambda d: y_high[zo + d])
        rows[12 + CY : 24 + CY] = jnp.zeros((12, NX), F32)
        total = stencil(lambda d: rows[5 + d : 5 + d + FY]) * keep_y
        if zo == 0:
            total = total * jnp.where(p > 0, 1.0, 0.0)
        elif zo >= 1 + CZ:
            total = total * jnp.where(p < SLABS - 1, 1.0, 0.0)
        for piece in range(NX // 128):
            at = 128 * piece
            wide[1 + piece, pl.ds(zo, FY, stride=FZ), :] = total[:, at : at + 128]
    for zo in range(CZ + 3, FZ):
        for piece in range(NX // 128):
            wide[1 + piece, pl.ds(zo, FY, stride=FZ), :] = jnp.zeros((FY, 128), F32)
    lane = lax.broadcasted_iota(jnp.int32, (32, FX), 1)
    inside = (lane >= 1) & (lane <= NX)

    def step(i, carry):
        at = pl.ds(pl.multiple_of(32 * i, 32), 32)
        values = jnp.concatenate([wide[c, at, :] for c in range(2 + NX // 128)], axis=1)
        total = stencil(lambda d: pltpu.roll(values, NX + 256 - 125 - d, 1)[:, :FX])
        out[at, :] = jnp.where(inside, total, 0.0)
        return carry

    lax.fori_loop(0, FY * FZ // 32, step, 0)


def spline_pair(distance):
    outer = jnp.maximum(2.0 - jnp.abs(distance), 0.0)
    inner = jnp.maximum(outer - 1.0, 0.0)
    outer_square = outer * outer
    inner_square = 4.0 * (inner * inner)
    value = outer_square * outer - inner_square * inner
    slope = inner_square - outer_square
    return value, jnp.where(distance < 0.0, -slope, slope)


def atoms_kernel(
    place, cell, count, near, arrived, x_high, x_low, along_y, along_z, offset, out, table, top
):
    top_high, top_low = split(arrived[...].T)
    potential = dot3(top_high, top_low, x_high[...], x_low[...])
    high, low = split(potential)
    top[0:128] = high
    top[128:256] = low
    lane = lax.broadcasted_iota(jnp.int32, (128, 128), 1)

    def build(i, carry):
        at = pl.ds(pl.multiple_of(128 * i, 128), 128)
        weight_high, weight_low = split(along_y[0, at, :].astype(F32) * along_z[0])
        fine = near[at, :] + dot3(weight_high, weight_low, top[0:128], top[128:256])
        fine_high = fine.astype(BF16).astype(F32)
        fine_low = fine - fine_high
        for t in range(TILES):
            shift = (FX - 32 * t) % FX
            a = pltpu.roll(fine_high, shift, 1)[:, :128]
            b = pltpu.roll(fine_low, (shift + TILE) % FX, 1)[:, :128]
            c = pltpu.roll(a, 2 * TILE, 1)
            row = jnp.where(lane < TILE, a, jnp.where(lane < 2 * TILE, b, c))
            table[t, at, :] = jnp.where(lane < 3 * TILE, row, 0.0).astype(BF16)
        return carry

    lax.fori_loop(0, FY * FZ // 128, build, 0)

    row16 = lax.broadcasted_iota(jnp.int32, (16, 128), 0).astype(F32) - 1.0
    row40 = lax.broadcasted_iota(jnp.int32, (TILE, 128), 0).astype(F32) - 1.0
    slot = lax.broadcasted_iota(jnp.int32, (1, 128), 1)
    blank = jnp.zeros((8, 256), F32)

    def block(b):
        at = pl.ds(pl.multiple_of(SLOT * b, SLOT), SLOT)
        t = cell[b]
        brick_y = lax.shift_right_logical(t, 6) & 7
        tile = lax.shift_right_logical(t, 2) & 15
        inner = (t & 3) * 8
        here = offset[:, at]
        wz, sz = spline_pair(here[0:1] - row16)
        wy, sy = spline_pair(here[1:2] - row16)
        wx, sx = spline_pair((here[2:3] + inner.astype(F32)) - row40)
        both = jnp.concatenate([wx, sx], axis=1)
        both_high = both.astype(BF16).astype(F32)
        weights = jnp.concatenate([both_high, both_high, both - both_high, blank], axis=0)
        first = pl.multiple_of(128 * brick_y, 128)
        patch = table[tile, pl.ds(first, 11 * FZ), :]
        product = dot(patch, weights.astype(BF16))
        base = along = cross = None
        for j in range(11):
            v = product[FZ * j : FZ * (j + 1), :128]
            d = product[FZ * j : FZ * (j + 1), 128:]
            w, s = wy[j : j + 1], sy[j : j + 1]
            base = v * w if base is None else base + v * w
            along = v * s if along is None else along + v * s
            cross = d * w if cross is None else cross + d * w

        def reduce(values):
            return jnp.sum(values, axis=0, keepdims=True)

        live = jnp.where(slot < count[b], 1.0, 0.0)
        slope = live * (-1.0 / 72.0)
        out[:, at] = jnp.concatenate(
            [
                reduce(base * wz) * (live * (1.0 / 216.0)),
                reduce(base * sz) * slope,
                reduce(along * wz) * slope,
                reduce(cross * wz) * slope,
            ],
            axis=0,
        )

    def step(i, carry):
        for k in range(4):
            block(4 * i + k)
        return carry

    lax.fori_loop(0, BLOCKS // 4, step, 0)


def whole(shape):
    return pl.BlockSpec(shape, lambda i, *_: (0,) * len(shape))


def call(kernel, scalars, in_specs, out_spec, out_shape, scratch, megabytes, flops, moved):
    return pl.pallas_call(
        kernel,
        grid_spec=pltpu.PrefetchScalarGridSpec(
            num_scalar_prefetch=scalars,
            grid=(1,),
            in_specs=in_specs,
            out_specs=out_spec,
            scratch_shapes=scratch,
        ),
        out_shape=jax.ShapeDtypeStruct(out_shape, F32),
        compiler_params=pltpu.CompilerParams(vmem_limit_bytes=megabytes * 2**20),
        cost_estimate=pl.CostEstimate(flops=flops, bytes_accessed=moved, transcendentals=0),
    )


def on_device(charge_grid, atom_offset, block_cell, block_count):
    consts = CONSTANTS
    p, q = lax.axis_index("slab"), lax.axis_index("sub")
    kind = jnp.where(p == 0, 0, jnp.where(p == SLABS - 1, 2, 1))
    place = jnp.stack([p, q, kind, kind * SUBS + q]).astype(jnp.int32)

    up = [(i, i + 1) for i in range(SLABS - 1)]
    down = [(b, a) for a, b in up]
    up_sub = [(i, i + 1) for i in range(SUBS - 1)]
    down_sub = [(b, a) for a, b in up_sub]

    partial = call(
        restrict_kernel,
        1,
        [
            whole((CZ, CY, NX)),
            whole((NX, 128)),
            pl.BlockSpec((1, CZ * CY, 128), lambda i, place: (place[3], 0, 0)),
        ],
        whole((128, 128)),
        (128, 128),
        [],
        32,
        2 * 10**8,
        2 * 10**6,
    )(place, charge_grid, consts["restrict_x"], consts["restrict_zy"])
    pencil = lax.all_to_all(partial, "slab", 0, 0, tiled=True)
    others = [
        lax.ppermute(pencil, "sub", [(i, (i + k) % SUBS) for i in range(SUBS)]) for k in (1, 2, 3)
    ]
    y_high, y_low = consts["span_y"]
    z_high, z_low = consts["span_z"]
    by_sub = pl.BlockSpec((1, 128, 384), lambda i, place: (place[1], 0, 0))
    folded = call(
        middle_kernel,
        1,
        [whole((128, 128))] * 4 + [by_sub, by_sub, whole((320, 384)), whole((320, 384))],
        whole((512, 128)),
        (512, 128),
        [],
        32,
        2 * 10**8,
        2 * 10**6,
    )(place, pencil, *others, y_high, y_low, z_high, z_low)
    arrived = lax.all_to_all(folded, "slab", 0, 0, tiled=True)

    below = lax.ppermute(charge_grid[CZ - 3 :], "slab", up)
    above = lax.ppermute(charge_grid[:4], "slab", down)
    left = jnp.concatenate([below[:, CY - 4 :], charge_grid[:, CY - 4 :], above[:, CY - 4 :]], axis=0)
    right = jnp.concatenate([below[:, :4], charge_grid[:, :4], above[:, :4]], axis=0)
    left = lax.ppermute(left, "sub", up_sub)
    right = lax.ppermute(right, "sub", down_sub)
    near = call(
        near_kernel,
        1,
        [
            whole((CZ, CY, NX)),
            whole((3, CY, NX)),
            whole((4, CY, NX)),
            whole((15, 4, NX)),
            whole((15, 4, NX)),
        ],
        whole((FY * FZ, FX)),
        (FY * FZ, FX),
        [pltpu.VMEM((CY + 24, NX), F32), pltpu.VMEM((2 + NX // 128, FY * FZ, 128), F32)],
        40,
        2 * 10**9,
        16 * 10**6,
    )(place, charge_grid, below, above, left, right)

    x_high, x_low = consts["fine_x"]
    return call(
        atoms_kernel,
        3,
        [
            whole((FY * FZ, FX)),
            whole((512, 128)),
            whole((512, FX)),
            whole((512, FX)),
            pl.BlockSpec((1, FY * FZ, 128), lambda i, place, *_: (place[1], 0, 0)),
            pl.BlockSpec((1, 128, 128), lambda i, place, *_: (place[2], 0, 0)),
            whole((3, BLOCKS * SLOT)),
        ],
        whole((4, BLOCKS * SLOT)),
        (4, BLOCKS * SLOT),
        [pltpu.VMEM((TILES, FY * FZ, 128), BF16), pltpu.VMEM((256, FX), BF16)],
        48,
        10**9,
        8 * 10**6,
    )(
        place,
        block_cell,
        block_count,
        near,
        arrived,
        x_high,
        x_low,
        consts["prolong_y"],
        consts["prolong_z"],
        atom_offset,
    )


def solution(mesh):
    placed = (
        P("slab", "sub", None),
        P(None, ("slab", "sub")),
        P(("slab", "sub")),
        P(("slab", "sub")),
    )
    return jax.shard_map(
        on_device, mesh=mesh, in_specs=placed, out_specs=P(None, ("slab", "sub")), check_vma=False
    )
```

```python
import math

import jax
import jax.numpy as jnp
import ml_dtypes
import numpy as np
from jax import lax
from jax.experimental import pallas as pl
from jax.experimental.pallas import tpu as pltpu
from jax.sharding import PartitionSpec as P

TAPS = (0.125, 0.5, 0.75, 0.5, 0.125)
SPANS = (2.0, 8.0, 32.0)
NEAR = [math.exp(-0.5 * d * d) for d in range(3)]
NEAR_WEIGHT = 0.5

SLABS, SUBS = 64, 4
CZ, CY, NX = 8, 64, 512
NZ, NY = CZ * SLABS, CY * SUBS
BLOCKS, SLOT = 128, 128

FZ, FY, FX = 16, 72, 640
TZ, TY, TYS = 5, 19, 24
GS = 21
TILE = 40
TILES = 16

F32, BF16 = jnp.float32, jnp.bfloat16


def restriction(n):
    matrix = np.zeros((n // 2, n))
    for target in range(n // 2):
        for offset in range(-2, 3):
            if 0 <= 2 * target + offset < n:
                matrix[target, 2 * target + offset] = TAPS[offset + 2]
    return matrix


def restriction_twice(n):
    return restriction(n // 2) @ restriction(n)


def gauss(n, span):
    index = np.arange(n, dtype=np.float64)
    return np.exp(-(((index[:, None] - index[None, :]) / span) ** 2))


def window(matrix, row0, rows, col0, cols):
    out = np.zeros((rows, cols))
    for r in range(rows):
        for c in range(cols):
            if 0 <= row0 + r < matrix.shape[0] and 0 <= col0 + c < matrix.shape[1]:
                out[r, c] = matrix[row0 + r, col0 + c]
    return out


def halves(matrix):
    whole = np.asarray(matrix, np.float32)
    high = whole.astype(ml_dtypes.bfloat16)
    low = (whole - high.astype(np.float32)).astype(ml_dtypes.bfloat16)
    return high, low


def split(values):
    high = values.astype(BF16)
    return high, (values - high.astype(F32)).astype(BF16)


def dot(left, right):
    return jnp.dot(left, right, preferred_element_type=F32)


def dot3(left_high, left_low, right_high, right_low):
    return dot(left_high, right_high) + (dot(left_low, right_high) + dot(left_high, right_low))


SLAB_KINDS = (0, 1, SLABS - 1)


def make_constants():
    rz, ry, rx = restriction_twice(NZ), restriction_twice(NY), restriction_twice(NX)
    restrict_x = rx.T.astype(ml_dtypes.bfloat16)
    restrict_zy = np.zeros((3, SUBS, CZ, CY, 128))
    for kind, p in enumerate(SLAB_KINDS):
        mz = window(rz, 2 * p - 1, TZ, CZ * p, CZ)
        for q in range(SUBS):
            my = window(ry, 16 * q - 1, TY, CY * q, CY)
            for zt in range(TZ):
                restrict_zy[kind, q, :, :, zt * TYS : zt * TYS + TY] = (
                    mz[zt][:, None, None] * my.T[None, :, :]
                )
    restrict_zy = restrict_zy.reshape(3 * SUBS, CZ * CY, 128).astype(np.float32)

    span_y = np.zeros((SUBS, 128, 3 * 128))
    span_z = np.zeros((TZ, SLABS, 3, 2, SLABS))
    fine_x = np.zeros((SLABS, 8, FX))
    for s, span in enumerate(SPANS):
        gy, gz, gx = gauss(NY // 4, span), gauss(NZ // 4, span), gauss(NX // 4, span)
        for q in range(SUBS):
            part = window(gy, 16 * q - 1, TY, 0, NY // 4).T
            for x in range(2):
                col = s * 128 + (s * 2 + x) * GS
                span_y[q, x * 64 : x * 64 + 64, col : col + TY] = part
        wide = np.zeros((NZ // 4 + 8, NZ // 4))
        wide[1 : 1 + NZ // 4] = gz * span ** (-1.5)
        for k in range(TZ):
            rows = wide[k : k + NZ // 4 : 2]
            span_z[k, :, s] = rows.reshape(SLABS, SLABS, 2).transpose(0, 2, 1)
        px = rx.T @ gx
        for x in range(2):
            fine_x[:, s * 2 + x, 1 : 1 + NX] = px[:, x::2].T
    span_z = span_z.reshape(TZ * SLABS, 3 * 128)
    fine_x = fine_x.reshape(SLABS * 8, FX)

    prolong_y = np.zeros((SUBS, FY, FZ, 128))
    for q in range(SUBS):
        part = window(ry.T, CY * q - 1, CY + 3, 16 * q - 1, TY)
        for zo in range(TZ):
            prolong_y[q, : CY + 3, :, zo * TYS : zo * TYS + TY] = part[:, None, :]
    prolong_y = prolong_y.reshape(SUBS, FY * FZ, 128).astype(ml_dtypes.bfloat16)
    prolong_z = np.zeros((3, 8, FZ, 128))
    for kind, p in enumerate(SLAB_KINDS):
        part = window(rz.T, CZ * p - 1, CZ + 3, 2 * p - 1, TZ)
        for zo in range(TZ):
            prolong_z[kind, :, : CZ + 3, zo * TYS : zo * TYS + TY] = part[None, :, zo, None]
    prolong_z = prolong_z.reshape(3, 8 * FZ, 128).astype(np.float32)
    near_x = np.zeros((NX, FX))
    for node in range(NX):
        for offset in range(-2, 3):
            if 0 <= node + offset < NX:
                near_x[node + offset, node + 1] = NEAR_WEIGHT * NEAR[abs(offset)]
    return dict(
        near_x=halves(near_x),
        restrict_x=restrict_x,
        restrict_zy=restrict_zy,
        span_y=halves(span_y),
        span_z=halves(span_z),
        fine_x=halves(fine_x),
        prolong_y=prolong_y,
        prolong_z=prolong_z,
    )


CONSTANTS = make_constants()


def restrict_kernel(place, charge, along_x, along_zy, out, first_planes, last_planes):
    first_planes[...] = charge[0:4]
    last_planes[...] = charge[CZ - 3 : CZ]
    values = charge[...].reshape(CZ * CY, NX)
    high, low = split(values)
    narrow = dot(high, along_x[...]) + dot(low, along_x[...])
    narrow_high, narrow_low = split(narrow.T)
    zy_high, zy_low = split(along_zy[0])
    out[...] = dot3(narrow_high, narrow_low, zy_high, zy_low)


def middle_kernel(place, own, one, two, three, y_high, y_low, z_high, z_low, out):
    q = place[1]
    lane = lax.broadcasted_iota(jnp.int32, (SLABS, 128), 1)
    gathered = [None] * TZ
    for back, ref in enumerate((own, one, two, three)):
        source = lax.rem(q + (SUBS - back), SUBS)
        for x in range(2):
            rows = ref[pl.ds(x, SLABS, stride=2), :]
            first = 64 * x - 1 + 16 * source
            inside = (lane >= first) & (lane < first + TY)
            for zt in range(TZ):
                shift = lax.rem(first + (256 - TYS * zt), 128)
                term = jnp.where(inside, pltpu.roll(rows, shift, 1), 0.0)
                gathered[zt] = term if gathered[zt] is None else gathered[zt] + term
    even = gathered[1] + pltpu.roll(gathered[3], 1, 0)
    odd = gathered[2] + pltpu.roll(gathered[4], 1, 0) + pltpu.roll(gathered[0], SLABS - 1, 0)
    top_high, top_low = split(jnp.concatenate([even, odd], axis=0))
    mixed = dot3(top_high, top_low, y_high[0], y_low[0])
    stacked = jnp.concatenate([mixed[:, :128], mixed[:, 128:256], mixed[:, 256:]], axis=0)
    stacked_high, stacked_low = split(stacked)
    folded = dot3(z_high[...], z_low[...], stacked_high, stacked_low)
    for g in range(6):
        total = None
        for k in range(TZ):
            piece = folded[k * SLABS : (k + 1) * SLABS]
            moved = pltpu.roll(piece, (256 + TYS * k - GS * g) % 128, 1)
            term = jnp.where((lane >= TYS * k) & (lane < TYS * k + TY), moved, 0.0)
            total = term if total is None else total + term
        out[pl.ds(g, SLABS, stride=8), :] = total
    for g in range(6, 8):
        out[pl.ds(g, SLABS, stride=8), :] = jnp.zeros((SLABS, 128), F32)


def near_kernel(place, charge, z_low, z_high, y_low, y_high, x_high, x_low, out, rows, wide):
    p, q = place[0], place[1]

    def stencil(at):
        return NEAR[2] * (at(0) + at(4)) + (NEAR[1] * (at(1) + at(3)) + at(2))

    def plane(k):
        if k < 3:
            return z_low[k]
        return charge[k - 3] if k < 3 + CZ else z_high[k - 3 - CZ]

    node = lax.broadcasted_iota(jnp.int32, (FY, 128), 0) + (CY * q - 1)
    keep_y = jnp.where((node >= 0) & (node < NY), 1.0, 0.0)
    keep_y = jnp.concatenate([keep_y] * (NX // 128), axis=1)
    for zo in range(CZ + 3):
        rows[8 : 8 + CY] = stencil(lambda d: plane(zo + d))
        rows[4:8] = stencil(lambda d: y_low[zo + d])
        rows[8 + CY : 12 + CY] = stencil(lambda d: y_high[zo + d])
        rows[12 + CY : 24 + CY] = jnp.zeros((12, NX), F32)
        total = stencil(lambda d: rows[5 + d : 5 + d + FY]) * keep_y
        if zo == 0:
            total = total * jnp.where(p > 0, 1.0, 0.0)
        elif zo >= 1 + CZ:
            total = total * jnp.where(p < SLABS - 1, 1.0, 0.0)
        for piece in range(NX // 128):
            at = 128 * piece
            wide[piece, pl.ds(zo, FY, stride=FZ), :] = total[:, at : at + 128]
    for zo in range(CZ + 3, FZ):
        for piece in range(NX // 128):
            wide[piece, pl.ds(zo, FY, stride=FZ), :] = jnp.zeros((FY, 128), F32)

    def step(i, carry):
        at = pl.ds(pl.multiple_of(128 * i, 128), 128)
        values = jnp.concatenate([wide[c, at, :] for c in range(NX // 128)], axis=1)
        high, low = split(values)
        out[at, :] = dot3(high, low, x_high[...], x_low[...])
        return carry

    lax.fori_loop(0, FY * FZ // 128, step, 0)


def spline_pair(distance):
    outer = jnp.maximum(2.0 - jnp.abs(distance), 0.0)
    inner = jnp.maximum(outer - 1.0, 0.0)
    outer_square = outer * outer
    inner_square = 4.0 * (inner * inner)
    value = outer_square * outer - inner_square * inner
    slope = inner_square - outer_square
    return value, jnp.where(distance < 0.0, -slope, slope)


def atoms_kernel(
    place, cell, count, near, arrived, x_high, x_low, along_y, along_z, offset, out, table, top
):
    top_high, top_low = split(arrived[...].T)
    potential = dot3(top_high, top_low, x_high[...], x_low[...])
    high, low = split(potential)
    top[0:128] = high
    top[128:256] = low
    lane = lax.broadcasted_iota(jnp.int32, (128, 128), 1)

    def build(i, carry):
        at = pl.ds(pl.multiple_of(128 * i, 128), 128)
        weight_high, weight_low = split(along_y[0, at, :].astype(F32) * along_z[0])
        fine = near[at, :] + dot3(weight_high, weight_low, top[0:128], top[128:256])
        fine_high = fine.astype(BF16).astype(F32)
        fine_low = fine - fine_high
        for t in range(TILES):
            tile, first = divmod(32 * t, 128)

            def moved(values, to):
                here = values[:, 128 * tile : 128 * tile + 128]
                here = pltpu.roll(here, (128 + to - first) % 128, 1) if to != first else here
                if first + TILE <= 128:
                    return here
                after = values[:, 128 * tile + 128 : 128 * tile + 256]
                after = pltpu.roll(after, (128 + to - first) % 128, 1)
                return jnp.where(lane < to + 128 - first, here, after)

            a = moved(fine_high, 0)
            b = moved(fine_low, TILE)
            c = pltpu.roll(a, 2 * TILE, 1)
            row = jnp.where(lane < TILE, a, jnp.where(lane < 2 * TILE, b, c))
            table[t, at, :] = row.astype(BF16)
        return carry

    lax.fori_loop(0, FY * FZ // 128, build, 0)

    row16 = lax.broadcasted_iota(jnp.int32, (16, 128), 0).astype(F32) - 1.0
    row40 = lax.broadcasted_iota(jnp.int32, (TILE, 128), 0).astype(F32) - 1.0
    slot = lax.broadcasted_iota(jnp.int32, (1, 128), 1)
    blank = jnp.zeros((8, 256), F32)

    def block(b):
        at = pl.ds(pl.multiple_of(SLOT * b, SLOT), SLOT)
        t = cell[b]
        brick_y = lax.shift_right_logical(t, 6) & 7
        tile = lax.shift_right_logical(t, 2) & 15
        inner = (t & 3) * 8
        here = offset[:, at]
        wz, sz = spline_pair(here[0:1] - row16)
        wy, sy = spline_pair(here[1:2] - row16)
        wx, sx = spline_pair((here[2:3] + inner.astype(F32)) - row40)
        both = jnp.concatenate([wx, sx], axis=1)
        both_high = both.astype(BF16).astype(F32)
        weights = jnp.concatenate([both_high, both_high, both - both_high, blank], axis=0)
        first = pl.multiple_of(128 * brick_y, 128)
        patch = table[tile, pl.ds(first, 11 * FZ), :]
        product = dot(patch, weights.astype(BF16))
        base = along = cross = None
        for j in range(11):
            v = product[FZ * j : FZ * (j + 1), :128]
            d = product[FZ * j : FZ * (j + 1), 128:]
            w, s = wy[j : j + 1], sy[j : j + 1]
            base = v * w if base is None else base + v * w
            along = v * s if along is None else along + v * s
            cross = d * w if cross is None else cross + d * w

        def reduce(values):
            return jnp.sum(values, axis=0, keepdims=True)

        live = jnp.where(slot < count[b], 1.0, 0.0)
        slope = live * (-1.0 / 72.0)
        out[:, at] = jnp.concatenate(
            [
                reduce(base * wz) * (live * (1.0 / 216.0)),
                reduce(base * sz) * slope,
                reduce(along * wz) * slope,
                reduce(cross * wz) * slope,
            ],
            axis=0,
        )

    def step(i, carry):
        for k in range(8):
            block(8 * i + k)
        return carry

    lax.fori_loop(0, BLOCKS // 8, step, 0)


def whole(shape):
    return pl.BlockSpec(shape, lambda i, *_: (0,) * len(shape))


def call(kernel, scalars, in_specs, out_spec, out_shape, scratch, megabytes, flops, moved):
    return pl.pallas_call(
        kernel,
        grid_spec=pltpu.PrefetchScalarGridSpec(
            num_scalar_prefetch=scalars,
            grid=(1,),
            in_specs=in_specs,
            out_specs=out_spec,
            scratch_shapes=scratch,
        ),
        out_shape=jax.tree.map(
            lambda shape: jax.ShapeDtypeStruct(shape, F32),
            out_shape,
            is_leaf=lambda shape: isinstance(shape, tuple),
        ),
        compiler_params=pltpu.CompilerParams(vmem_limit_bytes=megabytes * 2**20),
        cost_estimate=pl.CostEstimate(flops=flops, bytes_accessed=moved, transcendentals=0),
    )


def on_device(charge_grid, atom_offset, block_cell, block_count):
    consts = CONSTANTS
    p, q = lax.axis_index("slab"), lax.axis_index("sub")
    kind = jnp.where(p == 0, 0, jnp.where(p == SLABS - 1, 2, 1))
    place = jnp.stack([p, q, kind, kind * SUBS + q]).astype(jnp.int32)

    up = [(i, i + 1) for i in range(SLABS - 1)]
    down = [(b, a) for a, b in up]
    up_sub = [(i, i + 1) for i in range(SUBS - 1)]
    down_sub = [(b, a) for a, b in up_sub]

    partial, first_planes, last_planes = call(
        restrict_kernel,
        1,
        [
            whole((CZ, CY, NX)),
            whole((NX, 128)),
            pl.BlockSpec((1, CZ * CY, 128), lambda i, place: (place[3], 0, 0)),
        ],
        [whole((128, 128)), whole((4, CY, NX)), whole((3, CY, NX))],
        [(128, 128), (4, CY, NX), (3, CY, NX)],
        [],
        60,
        2 * 10**8,
        2 * 10**6,
    )(place, charge_grid, consts["restrict_x"], consts["restrict_zy"])
    pencil = lax.all_to_all(partial, "slab", 0, 0, tiled=True)
    others = [
        lax.ppermute(pencil, "sub", [(i, (i + k) % SUBS) for i in range(SUBS)]) for k in (1, 2, 3)
    ]
    y_high, y_low = consts["span_y"]
    z_high, z_low = consts["span_z"]
    by_sub = pl.BlockSpec((1, 128, 384), lambda i, place: (place[1], 0, 0))
    folded = call(
        middle_kernel,
        1,
        [whole((128, 128))] * 4 + [by_sub, by_sub, whole((320, 384)), whole((320, 384))],
        whole((512, 128)),
        (512, 128),
        [],
        32,
        2 * 10**8,
        2 * 10**6,
    )(place, pencil, *others, y_high, y_low, z_high, z_low)
    below = lax.ppermute(last_planes, "slab", up)
    above = lax.ppermute(first_planes, "slab", down)
    left = jnp.concatenate([below[:, CY - 4 :], charge_grid[:, CY - 4 :], above[:, CY - 4 :]], axis=0)
    right = jnp.concatenate([below[:, :4], charge_grid[:, :4], above[:, :4]], axis=0)
    left = lax.ppermute(left, "sub", up_sub)
    right = lax.ppermute(right, "sub", down_sub)
    left, right, folded = lax.optimization_barrier((left, right, folded))
    arrived = lax.all_to_all(folded, "slab", 0, 0, tiled=True)
    near = call(
        near_kernel,
        1,
        [
            whole((CZ, CY, NX)),
            whole((3, CY, NX)),
            whole((4, CY, NX)),
            whole((15, 4, NX)),
            whole((15, 4, NX)),
            whole((NX, FX)),
            whole((NX, FX)),
        ],
        whole((FY * FZ, FX)),
        (FY * FZ, FX),
        [pltpu.VMEM((CY + 24, NX), F32), pltpu.VMEM((NX // 128, FY * FZ, 128), F32)],
        60,
        2 * 10**9,
        16 * 10**6,
    )(place, charge_grid, below, above, left, right, *consts["near_x"])

    x_high, x_low = consts["fine_x"]
    return call(
        atoms_kernel,
        3,
        [
            whole((FY * FZ, FX)),
            whole((512, 128)),
            whole((512, FX)),
            whole((512, FX)),
            pl.BlockSpec((1, FY * FZ, 128), lambda i, place, *_: (place[1], 0, 0)),
            pl.BlockSpec((1, 128, 128), lambda i, place, *_: (place[2], 0, 0)),
            whole((3, BLOCKS * SLOT)),
        ],
        whole((4, BLOCKS * SLOT)),
        (4, BLOCKS * SLOT),
        [pltpu.VMEM((TILES, FY * FZ, 128), BF16), pltpu.VMEM((256, FX), BF16)],
        60,
        10**9,
        8 * 10**6,
    )(
        place,
        block_cell,
        block_count,
        near,
        arrived,
        x_high,
        x_low,
        consts["prolong_y"],
        consts["prolong_z"],
        atom_offset,
    )


def solution(mesh):
    placed = (
        P("slab", "sub", None),
        P(None, ("slab", "sub")),
        P(("slab", "sub")),
        P(("slab", "sub")),
    )
    return jax.shard_map(
        on_device, mesh=mesh, in_specs=placed, out_specs=P(None, ("slab", "sub")), check_vma=False
    )
```

```python
import math

import jax
import jax.numpy as jnp
import ml_dtypes
import numpy as np
from jax import lax
from jax.experimental import pallas as pl
from jax.experimental.pallas import tpu as pltpu
from jax.sharding import PartitionSpec as P

TAPS = (0.125, 0.5, 0.75, 0.5, 0.125)
SPANS = (2.0, 8.0, 32.0)
NEAR = [math.exp(-0.5 * d * d) for d in range(3)]
NEAR_WEIGHT = 0.5

SLABS, SUBS = 64, 4
CZ, CY, NX = 8, 64, 512
NZ, NY = CZ * SLABS, CY * SUBS
BLOCKS, SLOT = 128, 128

FZ, FY, FX = 16, 72, 640
TZ, TY, TYS = 5, 19, 24
GS = 21
TILE = 40
TILES = 16
ROWS = 384
STEP = 8

F32, BF16 = jnp.float32, jnp.bfloat16


def restriction(n):
    matrix = np.zeros((n // 2, n))
    for target in range(n // 2):
        for offset in range(-2, 3):
            if 0 <= 2 * target + offset < n:
                matrix[target, 2 * target + offset] = TAPS[offset + 2]
    return matrix


def restriction_twice(n):
    return restriction(n // 2) @ restriction(n)


def gauss(n, span):
    index = np.arange(n, dtype=np.float64)
    return np.exp(-(((index[:, None] - index[None, :]) / span) ** 2))


def window(matrix, row0, rows, col0, cols):
    out = np.zeros((rows, cols))
    for r in range(rows):
        for c in range(cols):
            if 0 <= row0 + r < matrix.shape[0] and 0 <= col0 + c < matrix.shape[1]:
                out[r, c] = matrix[row0 + r, col0 + c]
    return out


def halves(matrix):
    whole = np.asarray(matrix, np.float32)
    high = whole.astype(ml_dtypes.bfloat16)
    low = (whole - high.astype(np.float32)).astype(ml_dtypes.bfloat16)
    return high, low


def split(values):
    high = values.astype(BF16)
    return high, (values - high.astype(F32)).astype(BF16)


def dot(left, right):
    return jnp.dot(left, right, preferred_element_type=F32)


def dot3(left_high, left_low, right_high, right_low):
    return dot(left_high, right_high) + (dot(left_low, right_high) + dot(left_high, right_low))


SLAB_KINDS = (0, 1, SLABS - 1)


def make_constants():
    rz, ry, rx = restriction_twice(NZ), restriction_twice(NY), restriction_twice(NX)
    restrict_x = np.concatenate([rx[0::2], rx[1::2]]).T.astype(ml_dtypes.bfloat16)
    restrict_zy = np.zeros((3, SUBS, CZ, CY, 128))
    for kind, p in enumerate(SLAB_KINDS):
        mz = window(rz, 2 * p - 1, TZ, CZ * p, CZ)
        for q in range(SUBS):
            my = window(ry, 16 * q - 1, TY, CY * q, CY)
            for zt in range(TZ):
                restrict_zy[kind, q, :, :, zt * TYS : zt * TYS + TY] = (
                    mz[zt][:, None, None] * my.T[None, :, :]
                )
    restrict_zy = restrict_zy.reshape(3 * SUBS, CZ * CY, 128).astype(np.float32)

    span_y = np.zeros((SUBS, 128, 3 * 128))
    span_z = np.zeros((TZ, SLABS, 3, 2, SLABS))
    fine_x = np.zeros((SLABS, 8, FX))
    for s, span in enumerate(SPANS):
        gy, gz, gx = gauss(NY // 4, span), gauss(NZ // 4, span), gauss(NX // 4, span)
        for q in range(SUBS):
            part = window(gy, 16 * q - 1, TY, 0, NY // 4).T
            for x in range(2):
                col = s * 128 + (s * 2 + x) * GS
                span_y[q, x * 64 : x * 64 + 64, col : col + TY] = part
        wide = np.zeros((NZ // 4 + 8, NZ // 4))
        wide[1 : 1 + NZ // 4] = gz * span ** (-1.5)
        for k in range(TZ):
            rows = wide[k : k + NZ // 4 : 2]
            span_z[k, :, s] = rows.reshape(SLABS, SLABS, 2).transpose(0, 2, 1)
        px = rx.T @ gx
        for x in range(2):
            fine_x[:, s * 2 + x, 1 : 1 + NX] = px[:, x::2].T
    span_z = span_z.reshape(TZ * SLABS, 3 * 128)
    fine_x = fine_x.reshape(SLABS * 8, FX)

    prolong_y = np.zeros((SUBS, FY, FZ, 128))
    for q in range(SUBS):
        part = window(ry.T, CY * q - 1, CY + 3, 16 * q - 1, TY)
        for zo in range(TZ):
            prolong_y[q, : CY + 3, :, zo * TYS : zo * TYS + TY] = part[:, None, :]
    prolong_y = prolong_y.reshape(SUBS, FY * FZ, 128).astype(ml_dtypes.bfloat16)
    prolong_z = np.zeros((3, 8, FZ, 128))
    for kind, p in enumerate(SLAB_KINDS):
        part = window(rz.T, CZ * p - 1, CZ + 3, 2 * p - 1, TZ)
        for zo in range(TZ):
            prolong_z[kind, :, : CZ + 3, zo * TYS : zo * TYS + TY] = part[None, :, zo, None]
    prolong_z = prolong_z.reshape(3, 8 * FZ, 128).astype(ml_dtypes.bfloat16)
    near_x = np.zeros((NX, FX))
    for node in range(NX):
        for offset in range(-2, 3):
            if 0 <= node + offset < NX:
                near_x[node + offset, node + 1] = NEAR_WEIGHT * NEAR[abs(offset)]
    return dict(
        near_x=np.concatenate(halves(near_x)),
        restrict_x=restrict_x,
        restrict_zy=restrict_zy,
        span_y=halves(span_y),
        span_z=halves(span_z),
        fine_x=np.concatenate(halves(fine_x)),
        prolong_y=prolong_y,
        prolong_z=prolong_z,
    )


CONSTANTS = make_constants()


def restrict_kernel(place, charge, along_x, along_zy, source, out, first, last, sems):
    copies = [
        pltpu.make_async_copy(source.at[pl.ds(0, 4)], first, sems.at[0]),
        pltpu.make_async_copy(source.at[pl.ds(CZ - 3, 3)], last, sems.at[1]),
    ]
    for copy in copies:
        copy.start()
    values = charge[...].reshape(CZ * CY, NX)
    high, low = split(values)
    narrow = dot(high, along_x[...]) + dot(low, along_x[...])
    narrow_high, narrow_low = split(narrow.T)
    zy_high, zy_low = split(along_zy[0])
    partial = dot3(narrow_high, narrow_low, zy_high, zy_low)
    for x in range(2):
        for q in range(SUBS):
            out[pl.ds(2 * q + x, SLABS, stride=8), :] = partial[x * SLABS : (x + 1) * SLABS]
    for copy in copies:
        copy.wait()


def middle_kernel(place, pencil, y_high, y_low, z_high, z_low, out):
    q = place[1]
    lane = lax.broadcasted_iota(jnp.int32, (SLABS, 128), 1)
    gathered = [None] * TZ
    for source in range(SUBS):
        for x in range(2):
            rows = pencil[pl.ds(2 * source + x, SLABS, stride=8), :]
            first = 64 * x - 1 + 16 * source
            inside = (lane >= first) & (lane < first + TY)
            for zt in range(TZ):
                shift = (first + 256 - TYS * zt) % 128
                term = jnp.where(inside, pltpu.roll(rows, shift, 1), 0.0)
                gathered[zt] = term if gathered[zt] is None else gathered[zt] + term
    even = gathered[1] + pltpu.roll(gathered[3], 1, 0)
    odd = gathered[2] + pltpu.roll(gathered[4], 1, 0) + pltpu.roll(gathered[0], SLABS - 1, 0)
    top_high, top_low = split(jnp.concatenate([even, odd], axis=0))
    mixed = dot3(top_high, top_low, y_high[q], y_low[q])
    stacked = jnp.concatenate([mixed[:, :128], mixed[:, 128:256], mixed[:, 256:]], axis=0)
    stacked_high, stacked_low = split(stacked)
    folded = dot3(z_high[...], z_low[...], stacked_high, stacked_low)
    for g in range(6):
        total = None
        for k in range(TZ):
            piece = folded[k * SLABS : (k + 1) * SLABS]
            moved = pltpu.roll(piece, (256 + TYS * k - GS * g) % 128, 1)
            term = jnp.where((lane >= TYS * k) & (lane < TYS * k + TY), moved, 0.0)
            total = term if total is None else total + term
        out[pl.ds(g, SLABS, stride=8), :] = total
    for g in range(6, 8):
        out[pl.ds(g, SLABS, stride=8), :] = jnp.zeros((SLABS, 128), F32)


def fetch(sources, targets, sems):
    copies = [
        pltpu.make_async_copy(source, target, sems.at[i])
        for i, (source, target) in enumerate(zip(sources, targets))
    ]
    for copy in copies:
        copy.start()
    return copies


def near_kernel(
    place,
    charge_in,
    z_low_in,
    z_high_in,
    y_low_in,
    y_high_in,
    along_x_in,
    out,
    charge,
    z_low,
    z_high,
    y_low,
    y_high,
    along_x,
    rows,
    wide,
    grid,
    sems,
    out_sems,
):
    copies = fetch(
        (charge_in, z_low_in, z_high_in, y_low_in, y_high_in, along_x_in),
        (charge, z_low, z_high, y_low, y_high, along_x),
        sems,
    )
    for copy in copies[:5]:
        copy.wait()
    p, q = place[0], place[1]

    def stencil(at):
        return NEAR[2] * (at(0) + at(4)) + (NEAR[1] * (at(1) + at(3)) + at(2))

    def plane(k):
        if k < 3:
            return z_low[k]
        return charge[k - 3] if k < 3 + CZ else z_high[k - 3 - CZ]

    node = lax.broadcasted_iota(jnp.int32, (FY, 128), 0) + (CY * q - 1)
    keep_y = jnp.where((node >= 0) & (node < NY), 1.0, 0.0)
    keep_y = jnp.concatenate([keep_y] * (NX // 128), axis=1)
    for zo in range(CZ + 3):
        rows[8 : 8 + CY] = stencil(lambda d: plane(zo + d))
        rows[4:8] = stencil(lambda d: y_low[zo + d])
        rows[8 + CY : 12 + CY] = stencil(lambda d: y_high[zo + d])
        rows[12 + CY : 24 + CY] = jnp.zeros((12, NX), F32)
        total = stencil(lambda d: rows[5 + d : 5 + d + FY]) * keep_y
        if zo == 0:
            total = total * jnp.where(p > 0, 1.0, 0.0)
        elif zo >= 1 + CZ:
            total = total * jnp.where(p < SLABS - 1, 1.0, 0.0)
        for piece in range(NX // 128):
            at = 128 * piece
            wide[piece, pl.ds(zo, FY, stride=FZ), :] = total[:, at : at + 128]
    for zo in range(CZ + 3, FZ):
        for piece in range(NX // 128):
            wide[piece, pl.ds(zo, FY, stride=FZ), :] = jnp.zeros((FY, 128), F32)

    copies[5].wait()
    stores = []
    for i in range(FY * FZ // ROWS):
        at = pl.ds(ROWS * i, ROWS)
        values = jnp.concatenate([wide[c, at, :] for c in range(NX // 128)], axis=1)
        high, low = split(values)
        for k0, k1, n0, n1 in ((0, 384, 0, 256), (128, 512, 256, 512), (384, 512, 512, 640)):
            grid[at, n0:n1] = dot3(
                high[:, k0:k1],
                low[:, k0:k1],
                along_x[k0:k1, n0:n1],
                along_x[NX + k0 : NX + k1, n0:n1],
            )
        stores.append(pltpu.make_async_copy(grid.at[at], out.at[at], out_sems.at[i]))
        stores[-1].start()
    for store in stores:
        store.wait()


def spline_pair(distance):
    outer = jnp.maximum(2.0 - jnp.abs(distance), 0.0)
    inner = jnp.maximum(outer - 1.0, 0.0)
    outer_square = outer * outer
    inner_square = 4.0 * (inner * inner)
    value = outer_square * outer - inner_square * inner
    slope = inner_square - outer_square
    return value, jnp.where(distance < 0.0, -slope, slope)


def atoms_kernel(
    place,
    cell,
    count,
    arrived,
    near_in,
    along_x_in,
    along_y_in,
    along_z_in,
    offset_in,
    out,
    near,
    along_x,
    along_y,
    along_z,
    offset,
    table,
    grid,
    turned,
    fields,
    in_sems,
    sems,
):
    copies = fetch(
        (
            along_x_in,
            along_y_in.at[place[1]],
            along_z_in.at[place[2]],
            near_in,
            offset_in,
        ),
        (along_x, along_y, along_z, near, offset),
        in_sems,
    )
    top_high, top_low = split(arrived[...].T)
    copies[0].wait()
    top = dot3(top_high, top_low, along_x[0:512], along_x[512:1024])
    high, low = split(top)
    twice = jnp.concatenate([high, high], axis=0)
    for copy in copies[1:]:
        copy.wait()
    z_weight = jnp.concatenate([along_z[...].astype(F32)] * (ROWS // 128), axis=0)
    for i in range(FY * FZ // ROWS):
        at = pl.ds(ROWS * i, ROWS)
        weight_high, weight_low = split(along_y[at, :].astype(F32) * z_weight)
        both = jnp.concatenate([weight_high, weight_low], axis=1)
        grid[at, :] = near[at, :] + (dot(both, twice) + dot(weight_high, low))

    lane = lax.broadcasted_iota(jnp.int32, (32, 128), 1)

    def build(i, carry):
        at = pl.ds(pl.multiple_of(32 * i, 32), 32)
        values = grid[at, :]
        fine_high = values.astype(BF16).astype(F32)
        fine_low = values - fine_high
        h = [fine_high[:, 128 * c : 128 * c + 128] for c in range(5)]
        b = [pltpu.roll(fine_low[:, 128 * c : 128 * c + 128], TILE, 1) for c in range(5)]
        e = [pltpu.roll(h[c], 2 * TILE, 1) for c in range(5)]
        for c in range(4):
            for j in range(4):
                one, two, three = h[c], b[c], e[c]
                if j == 3:
                    one = jnp.where(lane < 64, h[c + 1], one)
                    two = jnp.where(lane >= TILE, b[c + 1], two)
                    three = jnp.where(lane >= 2 * TILE, e[c + 1], three)
                place_in = (lane + (128 - 32 * j)) & 127
                row = jnp.where(place_in < TILE, one, jnp.where(place_in < 2 * TILE, two, three))
                table[4 * c + j, at, :] = row.astype(BF16)
        return carry

    lax.fori_loop(0, (CY + 3) * FZ // 32 + 1, build, 0)

    row16 = lax.broadcasted_iota(jnp.int32, (16, 128), 0).astype(F32) - 1.0
    row40 = lax.broadcasted_iota(jnp.int32, (TILE, 128), 0).astype(F32) - 1.0
    slot = lax.broadcasted_iota(jnp.int32, (1, 128), 1)
    blank = jnp.zeros((8, 256), F32)

    def block(b, k):
        at = pl.ds(pl.multiple_of(SLOT * b, SLOT), SLOT)
        t = cell[b]
        brick_y = lax.shift_right_logical(t, 6) & 7
        tile = lax.shift_right_logical(t, 2) & 15
        inner = (t & 3) * 8
        here = offset[:, at]
        wz, sz = spline_pair(here[0:1] - row16)
        wy, sy = spline_pair(here[1:2] - row16)
        wx, sx = spline_pair((here[2:3] + inner.astype(F32)) - row40)
        both = jnp.concatenate([wx, sx], axis=1)
        both_high = both.astype(BF16).astype(F32)
        weights = jnp.concatenate([both_high, both_high, both - both_high, blank], axis=0)
        first = pl.multiple_of(128 * brick_y, 128)
        patch = table[tile, pl.ds(first, 11 * FZ), :]
        weights = weights.astype(BF16)
        turned[k, 0:128] = weights
        turned[k, 128:256] = weights
        turn = pl.multiple_of(128 - 32 * (tile & 3), 32)
        product = dot(patch, turned[k, pl.ds(turn, 128), :])
        base = along = cross = None
        for j in range(11):
            v = product[FZ * j : FZ * (j + 1), :128]
            d = product[FZ * j : FZ * (j + 1), 128:]
            w, s = wy[j : j + 1], sy[j : j + 1]
            base = v * w if base is None else base + v * w
            along = v * s if along is None else along + v * s
            cross = d * w if cross is None else cross + d * w

        def reduce(values):
            return jnp.sum(values, axis=0, keepdims=True)

        live = jnp.where(slot < count[b], 1.0, 0.0)
        slope = live * (-1.0 / 72.0)
        fields[:, at] = jnp.concatenate(
            [
                reduce(base * wz) * (live * (1.0 / 216.0)),
                reduce(base * sz) * slope,
                reduce(along * wz) * slope,
                reduce(cross * wz) * slope,
            ],
            axis=0,
        )

    def copy(i):
        at = pl.ds(pl.multiple_of(STEP * SLOT * i, STEP * SLOT), STEP * SLOT)
        return pltpu.make_async_copy(fields.at[:, at], out.at[:, at], sems.at[i])

    def step(i, carry):
        for k in range(STEP):
            block(STEP * i + k, k)
        copy(i).start()
        return carry

    lax.fori_loop(0, BLOCKS // STEP, step, 0)
    for i in range(BLOCKS // STEP):
        copy(i).wait()


def whole(shape):
    return pl.BlockSpec(shape, lambda i, *_: (0,) * len(shape))


IN_VMEM = pl.BlockSpec(memory_space=pltpu.VMEM)
IN_SMEM = pl.BlockSpec(memory_space=pltpu.SMEM)
ANYWHERE = pl.BlockSpec(memory_space=pl.ANY)


def call(kernel, scalars, near_by, far, out_shape, out_spec, scratch, megabytes, flops, moved):
    return pl.pallas_call(
        kernel,
        in_specs=[IN_SMEM] * len(scalars) + [IN_VMEM] * len(near_by) + [ANYWHERE] * len(far),
        out_specs=out_spec,
        out_shape=jax.ShapeDtypeStruct(out_shape, F32),
        scratch_shapes=scratch,
        compiler_params=pltpu.CompilerParams(vmem_limit_bytes=megabytes * 2**20),
        cost_estimate=pl.CostEstimate(flops=flops, bytes_accessed=moved, transcendentals=0),
    )(*scalars, *near_by, *far)


def on_device(charge_grid, atom_offset, block_cell, block_count):
    consts = CONSTANTS
    p, q = lax.axis_index("slab"), lax.axis_index("sub")
    kind = jnp.where(p == 0, 0, jnp.where(p == SLABS - 1, 2, 1))
    place = jnp.stack([p, q, kind, kind * SUBS + q]).astype(jnp.int32)

    up = [(i, i + 1) for i in range(SLABS - 1)]
    down = [(b, a) for a, b in up]
    up_sub = [(i, i + 1) for i in range(SUBS - 1)]
    down_sub = [(b, a) for a, b in up_sub]

    partial, first_planes, last_planes = pl.pallas_call(
        restrict_kernel,
        grid_spec=pltpu.PrefetchScalarGridSpec(
            num_scalar_prefetch=1,
            grid=(1,),
            in_specs=[
                whole((CZ, CY, NX)),
                whole((NX, 128)),
                pl.BlockSpec((1, CZ * CY, 128), lambda i, place: (place[3], 0, 0)),
                ANYWHERE,
            ],
            out_specs=[whole((512, 128)), ANYWHERE, ANYWHERE],
            scratch_shapes=[pltpu.SemaphoreType.DMA((2,))],
        ),
        out_shape=[
            jax.ShapeDtypeStruct((512, 128), F32),
            jax.ShapeDtypeStruct((4, CY, NX), F32),
            jax.ShapeDtypeStruct((3, CY, NX), F32),
        ],
        compiler_params=pltpu.CompilerParams(vmem_limit_bytes=60 * 2**20),
        cost_estimate=pl.CostEstimate(flops=10**8, bytes_accessed=10**6, transcendentals=0),
    )(place, charge_grid, consts["restrict_x"], consts["restrict_zy"], charge_grid)
    pencil = lax.all_to_all(partial, ("slab", "sub"), 0, 0, tiled=True)

    below = lax.ppermute(last_planes, "slab", up)
    above = lax.ppermute(first_planes, "slab", down)
    left = jnp.concatenate([below[:, CY - 4 :], charge_grid[:, CY - 4 :], above[:, CY - 4 :]], axis=0)
    right = jnp.concatenate([below[:, :4], charge_grid[:, :4], above[:, :4]], axis=0)
    left = lax.ppermute(left, "sub", up_sub)
    right = lax.ppermute(right, "sub", down_sub)
    pencil, left, right = lax.optimization_barrier((pencil, left, right))

    folded = call(
        middle_kernel,
        [place],
        [pencil, *consts["span_y"], *consts["span_z"]],
        [],
        (512, 128),
        IN_VMEM,
        [],
        12,
        2 * 10**8,
        2 * 10**6,
    )
    arrived = lax.all_to_all(folded, "slab", 0, 0, tiled=True)
    left, right, _ = lax.optimization_barrier((left, right, folded))
    near = call(
        near_kernel,
        [place],
        [],
        [charge_grid, below, above, left, right, consts["near_x"]],
        (FY * FZ, FX),
        ANYWHERE,
        [
            pltpu.VMEM((CZ, CY, NX), F32),
            pltpu.VMEM((3, CY, NX), F32),
            pltpu.VMEM((4, CY, NX), F32),
            pltpu.VMEM((15, 4, NX), F32),
            pltpu.VMEM((15, 4, NX), F32),
            pltpu.VMEM((2 * NX, FX), BF16),
            pltpu.VMEM((CY + 24, NX), F32),
            pltpu.VMEM((NX // 128, FY * FZ, 128), F32),
            pltpu.VMEM((FY * FZ, FX), F32),
            pltpu.SemaphoreType.DMA((6,)),
            pltpu.SemaphoreType.DMA((FY * FZ // ROWS,)),
        ],
        60,
        2 * 10**9,
        16 * 10**6,
    )
    return call(
        atoms_kernel,
        [place, block_cell, block_count],
        [arrived],
        [near, consts["fine_x"], consts["prolong_y"], consts["prolong_z"], atom_offset],
        (4, BLOCKS * SLOT),
        ANYWHERE,
        [
            pltpu.VMEM((FY * FZ, FX), F32),
            pltpu.VMEM((1024, FX), BF16),
            pltpu.VMEM((FY * FZ, 128), BF16),
            pltpu.VMEM((128, 128), BF16),
            pltpu.VMEM((3, BLOCKS * SLOT), F32),
            pltpu.VMEM((TILES, FY * FZ, 128), BF16),
            pltpu.VMEM((FY * FZ, FX), F32),
            pltpu.VMEM((STEP, 256, 256), BF16),
            pltpu.VMEM((4, BLOCKS * SLOT), F32),
            pltpu.SemaphoreType.DMA((5,)),
            pltpu.SemaphoreType.DMA((BLOCKS // STEP,)),
        ],
        60,
        10**9,
        8 * 10**6,
    )


def solution(mesh):
    placed = (
        P("slab", "sub", None),
        P(None, ("slab", "sub")),
        P(("slab", "sub")),
        P(("slab", "sub")),
    )
    return jax.shard_map(
        on_device, mesh=mesh, in_specs=placed, out_specs=P(None, ("slab", "sub")), check_vma=False
    )
```

```python
import math

import jax
import jax.numpy as jnp
import ml_dtypes
import numpy as np
from jax import lax
from jax.experimental import pallas as pl
from jax.experimental.pallas import tpu as pltpu
from jax.sharding import PartitionSpec as P

TAPS = (0.125, 0.5, 0.75, 0.5, 0.125)
SPANS = (2.0, 8.0, 32.0)
NEAR = [math.exp(-0.5 * d * d) for d in range(3)]
NEAR_WEIGHT = 0.5

SLABS, SUBS = 64, 4
CZ, CY, NX = 8, 64, 512
NZ, NY = CZ * SLABS, CY * SUBS
BLOCKS, SLOT = 128, 128

FZ, FY, FX = 16, 72, 640
TZ, TY, TYS = 5, 19, 24
GS = 21
TILE = 40
TILES = 16
ROWS = 384
STEP = 8

F32, BF16 = jnp.float32, jnp.bfloat16


def restriction(n):
    matrix = np.zeros((n // 2, n))
    for target in range(n // 2):
        for offset in range(-2, 3):
            if 0 <= 2 * target + offset < n:
                matrix[target, 2 * target + offset] = TAPS[offset + 2]
    return matrix


def restriction_twice(n):
    return restriction(n // 2) @ restriction(n)


def gauss(n, span):
    index = np.arange(n, dtype=np.float64)
    return np.exp(-(((index[:, None] - index[None, :]) / span) ** 2))


def window(matrix, row0, rows, col0, cols):
    out = np.zeros((rows, cols))
    for r in range(rows):
        for c in range(cols):
            if 0 <= row0 + r < matrix.shape[0] and 0 <= col0 + c < matrix.shape[1]:
                out[r, c] = matrix[row0 + r, col0 + c]
    return out


def halves(matrix):
    whole = np.asarray(matrix, np.float32)
    high = whole.astype(ml_dtypes.bfloat16)
    low = (whole - high.astype(np.float32)).astype(ml_dtypes.bfloat16)
    return high, low


def split(values):
    high = values.astype(BF16)
    return high, (values - high.astype(F32)).astype(BF16)


def dot(left, right):
    return jnp.dot(left, right, preferred_element_type=F32)


def dot3(left_high, left_low, right_high, right_low):
    return dot(left_high, right_high) + (dot(left_low, right_high) + dot(left_high, right_low))


SLAB_KINDS = (0, 1, SLABS - 1)


def make_constants():
    rz, ry, rx = restriction_twice(NZ), restriction_twice(NY), restriction_twice(NX)
    restrict_x = np.concatenate([rx[0::2], rx[1::2]]).T.astype(ml_dtypes.bfloat16)
    restrict_zy = np.zeros((3, SUBS, CZ, CY, 128))
    for kind, p in enumerate(SLAB_KINDS):
        mz = window(rz, 2 * p - 1, TZ, CZ * p, CZ)
        for q in range(SUBS):
            my = window(ry, 16 * q - 1, TY, CY * q, CY)
            for zt in range(TZ):
                restrict_zy[kind, q, :, :, zt * TYS : zt * TYS + TY] = (
                    mz[zt][:, None, None] * my.T[None, :, :]
                )
    restrict_zy = restrict_zy.reshape(3 * SUBS, CZ * CY, 128).astype(np.float32)

    span_y = np.zeros((SUBS, 128, 3 * 128))
    span_z = np.zeros((TZ, SLABS, 3, 2, SLABS))
    fine_x = np.zeros((SLABS, 8, FX))
    for s, span in enumerate(SPANS):
        gy, gz, gx = gauss(NY // 4, span), gauss(NZ // 4, span), gauss(NX // 4, span)
        for q in range(SUBS):
            part = window(gy, 16 * q - 1, TY, 0, NY // 4).T
            for x in range(2):
                col = s * 128 + (s * 2 + x) * GS
                span_y[q, x * 64 : x * 64 + 64, col : col + TY] = part
        wide = np.zeros((NZ // 4 + 8, NZ // 4))
        wide[1 : 1 + NZ // 4] = gz * span ** (-1.5)
        for k in range(TZ):
            rows = wide[k : k + NZ // 4 : 2]
            span_z[k, :, s] = rows.reshape(SLABS, SLABS, 2).transpose(0, 2, 1)
        px = rx.T @ gx
        for x in range(2):
            fine_x[:, s * 2 + x, 1 : 1 + NX] = px[:, x::2].T
    span_z = span_z.reshape(TZ * SLABS, 3 * 128)
    fine_x = fine_x.reshape(SLABS * 8, FX)

    prolong_y = np.zeros((SUBS, FY, FZ, 128))
    for q in range(SUBS):
        part = window(ry.T, CY * q - 1, CY + 3, 16 * q - 1, TY)
        for zo in range(TZ):
            prolong_y[q, : CY + 3, :, zo * TYS : zo * TYS + TY] = part[:, None, :]
    prolong_y = prolong_y.reshape(SUBS, FY * FZ, 128).astype(ml_dtypes.bfloat16)
    prolong_z = np.zeros((3, 8, FZ, 128))
    for kind, p in enumerate(SLAB_KINDS):
        part = window(rz.T, CZ * p - 1, CZ + 3, 2 * p - 1, TZ)
        for zo in range(TZ):
            prolong_z[kind, :, : CZ + 3, zo * TYS : zo * TYS + TY] = part[None, :, zo, None]
    prolong_z = prolong_z.reshape(3, 8 * FZ, 128).astype(ml_dtypes.bfloat16)
    near_x = np.zeros((NX, FX))
    for node in range(NX):
        for offset in range(-2, 3):
            if 0 <= node + offset < NX:
                near_x[node + offset, node + 1] = NEAR_WEIGHT * NEAR[abs(offset)]
    return dict(
        near_x=np.concatenate(halves(near_x)),
        restrict_x=restrict_x,
        restrict_zy=restrict_zy,
        span_y=halves(span_y),
        span_z=halves(span_z),
        fine_x=np.concatenate(halves(fine_x)),
        prolong_y=prolong_y,
        prolong_z=prolong_z,
    )


CONSTANTS = make_constants()


def restrict_kernel(place, charge, along_x, along_zy, out):
    values = charge[...].reshape(CZ * CY, NX)
    high, low = split(values)
    narrow = dot(high, along_x[...]) + dot(low, along_x[...])
    narrow_high, narrow_low = split(narrow.T)
    zy_high, zy_low = split(along_zy[0])
    partial = dot3(narrow_high, narrow_low, zy_high, zy_low)
    for x in range(2):
        for q in range(SUBS):
            out[pl.ds(2 * q + x, SLABS, stride=8), :] = partial[x * SLABS : (x + 1) * SLABS]


def middle_kernel(place, pencil, y_high, y_low, z_high, z_low, out):
    q = place[1]
    lane = lax.broadcasted_iota(jnp.int32, (SLABS, 128), 1)
    gathered = [None] * TZ
    for source in range(SUBS):
        for x in range(2):
            rows = pencil[pl.ds(2 * source + x, SLABS, stride=8), :]
            first = 64 * x - 1 + 16 * source
            inside = (lane >= first) & (lane < first + TY)
            for zt in range(TZ):
                shift = (first + 256 - TYS * zt) % 128
                term = jnp.where(inside, pltpu.roll(rows, shift, 1), 0.0)
                gathered[zt] = term if gathered[zt] is None else gathered[zt] + term
    even = gathered[1] + pltpu.roll(gathered[3], 1, 0)
    odd = gathered[2] + pltpu.roll(gathered[4], 1, 0) + pltpu.roll(gathered[0], SLABS - 1, 0)
    top_high, top_low = split(jnp.concatenate([even, odd], axis=0))
    mixed = dot3(top_high, top_low, y_high[q], y_low[q])
    stacked = jnp.concatenate([mixed[:, :128], mixed[:, 128:256], mixed[:, 256:]], axis=0)
    stacked_high, stacked_low = split(stacked)
    folded = dot3(z_high[...], z_low[...], stacked_high, stacked_low)
    for g in range(6):
        total = None
        for k in range(TZ):
            piece = folded[k * SLABS : (k + 1) * SLABS]
            moved = pltpu.roll(piece, (256 + TYS * k - GS * g) % 128, 1)
            term = jnp.where((lane >= TYS * k) & (lane < TYS * k + TY), moved, 0.0)
            total = term if total is None else total + term
        out[pl.ds(g, SLABS, stride=8), :] = total
    for g in range(6, 8):
        out[pl.ds(g, SLABS, stride=8), :] = jnp.zeros((SLABS, 128), F32)


def fetch(sources, targets, sems):
    copies = [
        pltpu.make_async_copy(source, target, sems.at[i])
        for i, (source, target) in enumerate(zip(sources, targets))
    ]
    for copy in copies:
        copy.start()
    return copies


def near_kernel(
    place,
    charge_in,
    z_low_in,
    z_high_in,
    y_low_in,
    y_high_in,
    along_x_in,
    out,
    charge,
    z_low,
    z_high,
    y_low,
    y_high,
    along_x,
    rows,
    wide,
    grid,
    sems,
    out_sems,
):
    copies = fetch(
        (charge_in, z_low_in.at[pl.ds(CZ - 3, 3)], z_high_in.at[pl.ds(0, 4)], y_low_in, y_high_in, along_x_in),
        (charge, z_low, z_high, y_low, y_high, along_x),
        sems,
    )
    for copy in copies[:5]:
        copy.wait()
    p, q = place[0], place[1]

    def stencil(at):
        return NEAR[2] * (at(0) + at(4)) + (NEAR[1] * (at(1) + at(3)) + at(2))

    def plane(k):
        if k < 3:
            return z_low[k]
        return charge[k - 3] if k < 3 + CZ else z_high[k - 3 - CZ]

    node = lax.broadcasted_iota(jnp.int32, (FY, 128), 0) + (CY * q - 1)
    keep_y = jnp.where((node >= 0) & (node < NY), 1.0, 0.0)
    keep_y = jnp.concatenate([keep_y] * (NX // 128), axis=1)
    for zo in range(CZ + 3):
        rows[8 : 8 + CY] = stencil(lambda d: plane(zo + d))
        rows[4:8] = stencil(lambda d: y_low[zo + d])
        rows[8 + CY : 12 + CY] = stencil(lambda d: y_high[zo + d])
        rows[12 + CY : 24 + CY] = jnp.zeros((12, NX), F32)
        total = stencil(lambda d: rows[5 + d : 5 + d + FY]) * keep_y
        if zo == 0:
            total = total * jnp.where(p > 0, 1.0, 0.0)
        elif zo >= 1 + CZ:
            total = total * jnp.where(p < SLABS - 1, 1.0, 0.0)
        for piece in range(NX // 128):
            at = 128 * piece
            wide[piece, pl.ds(zo, FY, stride=FZ), :] = total[:, at : at + 128]
    for zo in range(CZ + 3, FZ):
        for piece in range(NX // 128):
            wide[piece, pl.ds(zo, FY, stride=FZ), :] = jnp.zeros((FY, 128), F32)

    copies[5].wait()
    stores = []
    for i in range(FY * FZ // ROWS):
        at = pl.ds(ROWS * i, ROWS)
        values = jnp.concatenate([wide[c, at, :] for c in range(NX // 128)], axis=1)
        high, low = split(values)
        for k0, k1, n0, n1 in ((0, 384, 0, 256), (128, 512, 256, 512), (384, 512, 512, 640)):
            grid[at, n0:n1] = dot3(
                high[:, k0:k1],
                low[:, k0:k1],
                along_x[k0:k1, n0:n1],
                along_x[NX + k0 : NX + k1, n0:n1],
            )
        stores.append(pltpu.make_async_copy(grid.at[at], out.at[at], out_sems.at[i]))
        stores[-1].start()
    for store in stores:
        store.wait()


def spline_pair(distance):
    outer = jnp.maximum(2.0 - jnp.abs(distance), 0.0)
    inner = jnp.maximum(outer - 1.0, 0.0)
    outer_square = outer * outer
    inner_square = 4.0 * (inner * inner)
    value = outer_square * outer - inner_square * inner
    slope = inner_square - outer_square
    return value, jnp.where(distance < 0.0, -slope, slope)


def atoms_kernel(
    place,
    cell,
    count,
    arrived,
    near_in,
    along_x_in,
    along_y_in,
    along_z_in,
    offset_in,
    out,
    near,
    along_x,
    along_y,
    along_z,
    offset,
    table,
    grid,
    turned,
    fields,
    in_sems,
    sems,
):
    copies = fetch(
        (
            along_x_in,
            along_y_in.at[place[1]],
            along_z_in.at[place[2]],
            near_in,
            offset_in,
        ),
        (along_x, along_y, along_z, near, offset),
        in_sems,
    )
    top_high, top_low = split(arrived[...].T)
    copies[0].wait()
    top = dot3(top_high, top_low, along_x[0:512], along_x[512:1024])
    high, low = split(top)
    twice = jnp.concatenate([high, high], axis=0)
    for copy in copies[1:]:
        copy.wait()
    z_weight = jnp.concatenate([along_z[...].astype(F32)] * (ROWS // 128), axis=0)
    for i in range(FY * FZ // ROWS):
        at = pl.ds(ROWS * i, ROWS)
        weight_high, weight_low = split(along_y[at, :].astype(F32) * z_weight)
        both = jnp.concatenate([weight_high, weight_low], axis=1)
        grid[at, :] = near[at, :] + (dot(both, twice) + dot(weight_high, low))

    lane = lax.broadcasted_iota(jnp.int32, (32, 128), 1)

    def build(i, carry):
        at = pl.ds(pl.multiple_of(32 * i, 32), 32)
        values = grid[at, :]
        fine_high = values.astype(BF16).astype(F32)
        fine_low = values - fine_high
        h = [fine_high[:, 128 * c : 128 * c + 128] for c in range(5)]
        b = [pltpu.roll(fine_low[:, 128 * c : 128 * c + 128], TILE, 1) for c in range(5)]
        e = [pltpu.roll(h[c], 2 * TILE, 1) for c in range(5)]
        for c in range(4):
            for j in range(4):
                one, two, three = h[c], b[c], e[c]
                if j == 3:
                    one = jnp.where(lane < 64, h[c + 1], one)
                    two = jnp.where(lane >= TILE, b[c + 1], two)
                    three = jnp.where(lane >= 2 * TILE, e[c + 1], three)
                place_in = (lane + (128 - 32 * j)) & 127
                row = jnp.where(place_in < TILE, one, jnp.where(place_in < 2 * TILE, two, three))
                table[4 * c + j, at, :] = row.astype(BF16)
        return carry

    lax.fori_loop(0, (CY + 3) * FZ // 32 + 1, build, 0)

    row16 = lax.broadcasted_iota(jnp.int32, (16, 128), 0).astype(F32) - 1.0
    row40 = lax.broadcasted_iota(jnp.int32, (TILE, 128), 0).astype(F32) - 1.0
    slot = lax.broadcasted_iota(jnp.int32, (1, 128), 1)
    blank = jnp.zeros((8, 256), F32)

    def block(b, k):
        at = pl.ds(pl.multiple_of(SLOT * b, SLOT), SLOT)
        t = cell[b]
        brick_y = lax.shift_right_logical(t, 6) & 7
        tile = lax.shift_right_logical(t, 2) & 15
        inner = (t & 3) * 8
        here = offset[:, at]
        wz, sz = spline_pair(here[0:1] - row16)
        wy, sy = spline_pair(here[1:2] - row16)
        wx, sx = spline_pair((here[2:3] + inner.astype(F32)) - row40)
        both = jnp.concatenate([wx, sx], axis=1)
        both_high = both.astype(BF16).astype(F32)
        weights = jnp.concatenate([both_high, both_high, both - both_high, blank], axis=0)
        first = pl.multiple_of(128 * brick_y, 128)
        patch = table[tile, pl.ds(first, 11 * FZ), :]
        weights = weights.astype(BF16)
        turned[k, 0:128] = weights
        turned[k, 128:256] = weights
        turn = pl.multiple_of(128 - 32 * (tile & 3), 32)
        product = dot(patch, turned[k, pl.ds(turn, 128), :])
        base = along = cross = None
        for j in range(11):
            v = product[FZ * j : FZ * (j + 1), :128]
            d = product[FZ * j : FZ * (j + 1), 128:]
            w, s = wy[j : j + 1], sy[j : j + 1]
            base = v * w if base is None else base + v * w
            along = v * s if along is None else along + v * s
            cross = d * w if cross is None else cross + d * w

        def reduce(values):
            return jnp.sum(values, axis=0, keepdims=True)

        live = jnp.where(slot < count[b], 1.0, 0.0)
        slope = live * (-1.0 / 72.0)
        fields[:, at] = jnp.concatenate(
            [
                reduce(base * wz) * (live * (1.0 / 216.0)),
                reduce(base * sz) * slope,
                reduce(along * wz) * slope,
                reduce(cross * wz) * slope,
            ],
            axis=0,
        )

    def copy(i):
        at = pl.ds(pl.multiple_of(STEP * SLOT * i, STEP * SLOT), STEP * SLOT)
        return pltpu.make_async_copy(fields.at[:, at], out.at[:, at], sems.at[i])

    def step(i, carry):
        for k in range(STEP):
            block(STEP * i + k, k)
        copy(i).start()
        return carry

    lax.fori_loop(0, BLOCKS // STEP, step, 0)
    for i in range(BLOCKS // STEP):
        copy(i).wait()


def whole(shape):
    return pl.BlockSpec(shape, lambda i, *_: (0,) * len(shape))


IN_VMEM = pl.BlockSpec(memory_space=pltpu.VMEM)
IN_SMEM = pl.BlockSpec(memory_space=pltpu.SMEM)
ANYWHERE = pl.BlockSpec(memory_space=pl.ANY)


def call(kernel, scalars, near_by, far, out_shape, out_spec, scratch, megabytes, flops, moved):
    return pl.pallas_call(
        kernel,
        in_specs=[IN_SMEM] * len(scalars) + [IN_VMEM] * len(near_by) + [ANYWHERE] * len(far),
        out_specs=out_spec,
        out_shape=jax.ShapeDtypeStruct(out_shape, F32),
        scratch_shapes=scratch,
        compiler_params=pltpu.CompilerParams(vmem_limit_bytes=megabytes * 2**20),
        cost_estimate=pl.CostEstimate(flops=flops, bytes_accessed=moved, transcendentals=0),
    )(*scalars, *near_by, *far)


def on_device(charge_grid, atom_offset, block_cell, block_count):
    consts = CONSTANTS
    p, q = lax.axis_index("slab"), lax.axis_index("sub")
    kind = jnp.where(p == 0, 0, jnp.where(p == SLABS - 1, 2, 1))
    place = jnp.stack([p, q, kind, kind * SUBS + q]).astype(jnp.int32)

    up = [(i, i + 1) for i in range(SLABS - 1)]
    down = [(b, a) for a, b in up]
    up_sub = [(i, i + 1) for i in range(SUBS - 1)]
    down_sub = [(b, a) for a, b in up_sub]

    below = lax.ppermute(charge_grid, "slab", up)
    above = lax.ppermute(charge_grid, "slab", down)
    partial = pl.pallas_call(
        restrict_kernel,
        grid_spec=pltpu.PrefetchScalarGridSpec(
            num_scalar_prefetch=1,
            grid=(1,),
            in_specs=[
                whole((CZ, CY, NX)),
                whole((NX, 128)),
                pl.BlockSpec((1, CZ * CY, 128), lambda i, place: (place[3], 0, 0)),
            ],
            out_specs=whole((512, 128)),
        ),
        out_shape=jax.ShapeDtypeStruct((512, 128), F32),
        compiler_params=pltpu.CompilerParams(vmem_limit_bytes=60 * 2**20),
        cost_estimate=pl.CostEstimate(flops=10**8, bytes_accessed=10**6, transcendentals=0),
    )(place, charge_grid, consts["restrict_x"], consts["restrict_zy"])
    pencil = lax.all_to_all(partial, ("slab", "sub"), 0, 0, tiled=True)

    planes = (below[CZ - 3 :], charge_grid, above[:4])
    left = jnp.concatenate([plane[:, CY - 4 :] for plane in planes], axis=0)
    right = jnp.concatenate([plane[:, :4] for plane in planes], axis=0)
    left = lax.ppermute(left, "sub", up_sub)
    right = lax.ppermute(right, "sub", down_sub)
    pencil, left, right = lax.optimization_barrier((pencil, left, right))

    folded = call(
        middle_kernel,
        [place],
        [pencil, *consts["span_y"], *consts["span_z"]],
        [],
        (512, 128),
        IN_VMEM,
        [],
        12,
        2 * 10**8,
        2 * 10**6,
    )
    arrived = lax.all_to_all(folded, "slab", 0, 0, tiled=True)
    left, right, _ = lax.optimization_barrier((left, right, folded))
    near = call(
        near_kernel,
        [place],
        [],
        [charge_grid, below, above, left, right, consts["near_x"]],
        (FY * FZ, FX),
        ANYWHERE,
        [
            pltpu.VMEM((CZ, CY, NX), F32),
            pltpu.VMEM((3, CY, NX), F32),
            pltpu.VMEM((4, CY, NX), F32),
            pltpu.VMEM((15, 4, NX), F32),
            pltpu.VMEM((15, 4, NX), F32),
            pltpu.VMEM((2 * NX, FX), BF16),
            pltpu.VMEM((CY + 24, NX), F32),
            pltpu.VMEM((NX // 128, FY * FZ, 128), F32),
            pltpu.VMEM((FY * FZ, FX), F32),
            pltpu.SemaphoreType.DMA((6,)),
            pltpu.SemaphoreType.DMA((FY * FZ // ROWS,)),
        ],
        60,
        2 * 10**9,
        16 * 10**6,
    )
    return call(
        atoms_kernel,
        [place, block_cell, block_count],
        [arrived],
        [near, consts["fine_x"], consts["prolong_y"], consts["prolong_z"], atom_offset],
        (4, BLOCKS * SLOT),
        ANYWHERE,
        [
            pltpu.VMEM((FY * FZ, FX), F32),
            pltpu.VMEM((1024, FX), BF16),
            pltpu.VMEM((FY * FZ, 128), BF16),
            pltpu.VMEM((128, 128), BF16),
            pltpu.VMEM((3, BLOCKS * SLOT), F32),
            pltpu.VMEM((TILES, FY * FZ, 128), BF16),
            pltpu.VMEM((FY * FZ, FX), F32),
            pltpu.VMEM((STEP, 256, 256), BF16),
            pltpu.VMEM((4, BLOCKS * SLOT), F32),
            pltpu.SemaphoreType.DMA((5,)),
            pltpu.SemaphoreType.DMA((BLOCKS // STEP,)),
        ],
        60,
        10**9,
        8 * 10**6,
    )


def solution(mesh):
    placed = (
        P("slab", "sub", None),
        P(None, ("slab", "sub")),
        P(("slab", "sub")),
        P(("slab", "sub")),
    )
    return jax.shard_map(
        on_device, mesh=mesh, in_specs=placed, out_specs=P(None, ("slab", "sub")), check_vma=False
    )
```

```python
import math

import jax
import jax.numpy as jnp
import ml_dtypes
import numpy as np
from jax import lax
from jax.experimental import pallas as pl
from jax.experimental.pallas import tpu as pltpu
from jax.sharding import PartitionSpec as P

TAPS = (0.125, 0.5, 0.75, 0.5, 0.125)
SPANS = (2.0, 8.0, 32.0)
NEAR = [math.exp(-0.5 * d * d) for d in range(3)]
NEAR_WEIGHT = 0.5

SLABS, SUBS = 64, 4
CZ, CY, NX = 8, 64, 512
NZ, NY = CZ * SLABS, CY * SUBS
BLOCKS, SLOT = 128, 128

FZ, FY, FX = 16, 72, 640
TZ, TY, TYS = 5, 19, 24
GS = 21
TILE = 40
TILES = 16
ROWS = 384
STEP = 8

F32, BF16 = jnp.float32, jnp.bfloat16


def restriction(n):
    matrix = np.zeros((n // 2, n))
    for target in range(n // 2):
        for offset in range(-2, 3):
            if 0 <= 2 * target + offset < n:
                matrix[target, 2 * target + offset] = TAPS[offset + 2]
    return matrix


def restriction_twice(n):
    return restriction(n // 2) @ restriction(n)


def gauss(n, span):
    index = np.arange(n, dtype=np.float64)
    return np.exp(-(((index[:, None] - index[None, :]) / span) ** 2))


def window(matrix, row0, rows, col0, cols):
    out = np.zeros((rows, cols))
    for r in range(rows):
        for c in range(cols):
            if 0 <= row0 + r < matrix.shape[0] and 0 <= col0 + c < matrix.shape[1]:
                out[r, c] = matrix[row0 + r, col0 + c]
    return out


def far_nodes(n, first):
    natural = np.zeros(13)
    for outer in range(5):
        for inner in range(5):
            natural[2 * inner + outer] += TAPS[outer] * TAPS[inner]
    true = restriction_twice(n).T
    rows = np.zeros((8, n // 4))
    high = first + 8 == n
    for r in range(8):
        if r < 4 or (r == 4 and not high):
            cell = first // 4 + r - 1
            if 0 <= cell < n // 4:
                rows[r, cell] = 1.0
            continue
        at = first + (r + 2 if high else r - 6)
        if 0 <= at < n:
            rows[r] = true[at]
        for cell in range(n // 4):
            if abs(at - 4 * cell) <= 6:
                rows[r, cell] -= natural[at - 4 * cell + 6]
    return rows


def halves(matrix):
    whole = np.asarray(matrix, np.float32)
    high = whole.astype(ml_dtypes.bfloat16)
    low = (whole - high.astype(np.float32)).astype(ml_dtypes.bfloat16)
    return high, low


def split(values):
    high = values.astype(BF16)
    return high, (values - high.astype(F32)).astype(BF16)


def dot(left, right):
    return jnp.dot(left, right, preferred_element_type=F32)


def dot3(left_high, left_low, right_high, right_low):
    return dot(left_high, right_high) + (dot(left_low, right_high) + dot(left_high, right_low))


SLAB_KINDS = (0, 1, SLABS - 1)


def make_constants():
    rz, ry, rx = restriction_twice(NZ), restriction_twice(NY), restriction_twice(NX)
    restrict_x = np.concatenate([rx[0::2], rx[1::2]]).T.astype(ml_dtypes.bfloat16)
    restrict_zy = np.zeros((3, SUBS, CZ, CY, 128))
    for kind, p in enumerate(SLAB_KINDS):
        mz = window(rz, 2 * p - 1, TZ, CZ * p, CZ)
        for q in range(SUBS):
            my = window(ry, 16 * q - 1, TY, CY * q, CY)
            for zt in range(TZ):
                restrict_zy[kind, q, :, :, zt * TYS : zt * TYS + TY] = (
                    mz[zt][:, None, None] * my.T[None, :, :]
                )
    restrict_zy = restrict_zy.reshape(3 * SUBS, CZ * CY, 128).astype(np.float32)

    span_y = np.zeros((SUBS, 128, 3 * 128))
    span_z = np.zeros((TZ, SLABS, 3, 2, SLABS))
    far_x = np.zeros((SLABS, 8, NX))
    spread = np.concatenate([far_nodes(NX, 8 * brick) for brick in range(NX // 8)])
    order = np.arange(NX).reshape(4, 4, 4, 8).transpose(0, 2, 1, 3).reshape(NX)
    for s, span in enumerate(SPANS):
        gy, gz, gx = gauss(NY // 4, span), gauss(NZ // 4, span), gauss(NX // 4, span)
        for q in range(SUBS):
            part = window(gy, 16 * q - 1, TY, 0, NY // 4).T
            for x in range(2):
                col = s * 128 + (s * 2 + x) * GS
                span_y[q, x * 64 : x * 64 + 64, col : col + TY] = part
        wide = np.zeros((NZ // 4 + 8, NZ // 4))
        wide[1 : 1 + NZ // 4] = gz * span ** (-1.5)
        for k in range(TZ):
            rows = wide[k : k + NZ // 4 : 2]
            span_z[k, :, s] = rows.reshape(SLABS, SLABS, 2).transpose(0, 2, 1)
        px = (spread @ gx)[order]
        for x in range(2):
            far_x[:, s * 2 + x] = px[:, x::2].T
    span_z = span_z.reshape(TZ * SLABS, 3 * 128)
    far_x = far_x.reshape(SLABS * 8, NX)

    far_y = np.zeros((SUBS, CY // 8, 8, 8, 128))
    for q in range(SUBS):
        for brick in range(CY // 8):
            nodes = far_nodes(NY, CY * q + 8 * brick)
            part = window(nodes, 0, 8, 16 * q - 1, TY)
            for zo in range(TZ):
                far_y[q, brick, :, :, zo * TYS : zo * TYS + TY] = part[:, None, :]
    far_y = far_y.reshape(SUBS, 512, 128).astype(ml_dtypes.bfloat16)
    far_z = np.zeros((3, 8, 8, 128))
    for kind, p in enumerate(SLAB_KINDS):
        part = window(far_nodes(NZ, CZ * p), 0, 8, 2 * p - 1, TZ)
        for zo in range(TZ):
            far_z[kind, :, :, zo * TYS : zo * TYS + TY] = part[None, :, zo, None]
    far_z = far_z.reshape(3, 64, 128).astype(ml_dtypes.bfloat16)
    near_x = np.zeros((NX, FX))
    for node in range(NX):
        for offset in range(-2, 3):
            if 0 <= node + offset < NX:
                near_x[node + offset, node + 1] = NEAR_WEIGHT * NEAR[abs(offset)]
    return dict(
        near_x=np.concatenate(halves(near_x)),
        restrict_x=restrict_x,
        restrict_zy=restrict_zy,
        span_y=halves(span_y),
        span_z=halves(span_z),
        far_x=np.concatenate(halves(far_x)),
        far_y=far_y,
        far_z=far_z,
    )


CONSTANTS = make_constants()


def restrict_kernel(place, charge, along_x, along_zy, out):
    values = charge[...].reshape(CZ * CY, NX)
    high, low = split(values)
    narrow = dot(high, along_x[...]) + dot(low, along_x[...])
    narrow_high, narrow_low = split(narrow.T)
    zy_high, zy_low = split(along_zy[0])
    partial = dot3(narrow_high, narrow_low, zy_high, zy_low)
    for x in range(2):
        for q in range(SUBS):
            out[pl.ds(2 * q + x, SLABS, stride=8), :] = partial[x * SLABS : (x + 1) * SLABS]


def middle_kernel(place, pencil, y_high, y_low, z_high, z_low, out):
    q = place[1]
    lane = lax.broadcasted_iota(jnp.int32, (SLABS, 128), 1)
    gathered = [None] * TZ
    for source in range(SUBS):
        for x in range(2):
            rows = pencil[pl.ds(2 * source + x, SLABS, stride=8), :]
            first = 64 * x - 1 + 16 * source
            inside = (lane >= first) & (lane < first + TY)
            for zt in range(TZ):
                shift = (first + 256 - TYS * zt) % 128
                term = jnp.where(inside, pltpu.roll(rows, shift, 1), 0.0)
                gathered[zt] = term if gathered[zt] is None else gathered[zt] + term
    even = gathered[1] + pltpu.roll(gathered[3], 1, 0)
    odd = gathered[2] + pltpu.roll(gathered[4], 1, 0) + pltpu.roll(gathered[0], SLABS - 1, 0)
    top_high, top_low = split(jnp.concatenate([even, odd], axis=0))
    mixed = dot3(top_high, top_low, y_high[q], y_low[q])
    stacked = jnp.concatenate([mixed[:, :128], mixed[:, 128:256], mixed[:, 256:]], axis=0)
    stacked_high, stacked_low = split(stacked)
    folded = dot3(z_high[...], z_low[...], stacked_high, stacked_low)
    for g in range(6):
        total = None
        for k in range(TZ):
            piece = folded[k * SLABS : (k + 1) * SLABS]
            moved = pltpu.roll(piece, (256 + TYS * k - GS * g) % 128, 1)
            term = jnp.where((lane >= TYS * k) & (lane < TYS * k + TY), moved, 0.0)
            total = term if total is None else total + term
        out[pl.ds(g, SLABS, stride=8), :] = total
    for g in range(6, 8):
        out[pl.ds(g, SLABS, stride=8), :] = jnp.zeros((SLABS, 128), F32)


def fetch(sources, targets, sems):
    copies = [
        pltpu.make_async_copy(source, target, sems.at[i])
        for i, (source, target) in enumerate(zip(sources, targets))
    ]
    for copy in copies:
        copy.start()
    return copies


def near_kernel(
    place,
    charge_in,
    z_low_in,
    z_high_in,
    y_low_in,
    y_high_in,
    along_x_in,
    out,
    charge,
    z_low,
    z_high,
    y_low,
    y_high,
    along_x,
    rows,
    wide,
    grid,
    sems,
    out_sems,
):
    copies = fetch(
        (charge_in, z_low_in.at[pl.ds(CZ - 3, 3)], z_high_in.at[pl.ds(0, 4)], y_low_in, y_high_in, along_x_in),
        (charge, z_low, z_high, y_low, y_high, along_x),
        sems,
    )
    for copy in copies[:5]:
        copy.wait()
    p, q = place[0], place[1]

    def stencil(at):
        return NEAR[2] * (at(0) + at(4)) + (NEAR[1] * (at(1) + at(3)) + at(2))

    def plane(k):
        if k < 3:
            return z_low[k]
        return charge[k - 3] if k < 3 + CZ else z_high[k - 3 - CZ]

    node = lax.broadcasted_iota(jnp.int32, (FY, 128), 0) + (CY * q - 1)
    keep_y = jnp.where((node >= 0) & (node < NY), 1.0, 0.0)
    keep_y = jnp.concatenate([keep_y] * (NX // 128), axis=1)
    for zo in range(CZ + 3):
        rows[8 : 8 + CY] = stencil(lambda d: plane(zo + d))
        rows[4:8] = stencil(lambda d: y_low[zo + d])
        rows[8 + CY : 12 + CY] = stencil(lambda d: y_high[zo + d])
        rows[12 + CY : 24 + CY] = jnp.zeros((12, NX), F32)
        total = stencil(lambda d: rows[5 + d : 5 + d + FY]) * keep_y
        if zo == 0:
            total = total * jnp.where(p > 0, 1.0, 0.0)
        elif zo >= 1 + CZ:
            total = total * jnp.where(p < SLABS - 1, 1.0, 0.0)
        for piece in range(NX // 128):
            at = 128 * piece
            wide[piece, pl.ds(zo, FY, stride=FZ), :] = total[:, at : at + 128]
    for zo in range(CZ + 3, FZ):
        for piece in range(NX // 128):
            wide[piece, pl.ds(zo, FY, stride=FZ), :] = jnp.zeros((FY, 128), F32)

    copies[5].wait()
    stores = []
    for i in range(FY * FZ // ROWS):
        at = pl.ds(ROWS * i, ROWS)
        values = jnp.concatenate([wide[c, at, :] for c in range(NX // 128)], axis=1)
        high, low = split(values)
        for k0, k1, n0, n1 in ((0, 384, 0, 256), (128, 512, 256, 512), (384, 512, 512, 640)):
            grid[at, n0:n1] = dot3(
                high[:, k0:k1],
                low[:, k0:k1],
                along_x[k0:k1, n0:n1],
                along_x[NX + k0 : NX + k1, n0:n1],
            )
        stores.append(pltpu.make_async_copy(grid.at[at], out.at[at], out_sems.at[i]))
        stores[-1].start()
    for store in stores:
        store.wait()


def spline_pair(distance):
    outer = jnp.maximum(2.0 - jnp.abs(distance), 0.0)
    inner = jnp.maximum(outer - 1.0, 0.0)
    outer_square = outer * outer
    inner_square = 4.0 * (inner * inner)
    value = outer_square * outer - inner_square * inner
    slope = inner_square - outer_square
    return value, jnp.where(distance < 0.0, -slope, slope)


def atoms_kernel(cell, count, near_in, offset_in, out, grid, offset, table, turned, fields, in_sems, sems):
    copies = fetch((near_in, offset_in), (grid, offset), in_sems)
    for copy in copies:
        copy.wait()
    lane = lax.broadcasted_iota(jnp.int32, (32, 128), 1)

    def build(i, carry):
        at = pl.ds(pl.multiple_of(32 * i, 32), 32)
        values = grid[at, :]
        fine_high = values.astype(BF16).astype(F32)
        fine_low = values - fine_high
        h = [fine_high[:, 128 * c : 128 * c + 128] for c in range(5)]
        b = [pltpu.roll(fine_low[:, 128 * c : 128 * c + 128], TILE, 1) for c in range(5)]
        e = [pltpu.roll(h[c], 2 * TILE, 1) for c in range(5)]
        for c in range(4):
            for j in range(4):
                one, two, three = h[c], b[c], e[c]
                if j == 3:
                    one = jnp.where(lane < 64, h[c + 1], one)
                    two = jnp.where(lane >= TILE, b[c + 1], two)
                    three = jnp.where(lane >= 2 * TILE, e[c + 1], three)
                place_in = (lane + (128 - 32 * j)) & 127
                row = jnp.where(place_in < TILE, one, jnp.where(place_in < 2 * TILE, two, three))
                table[4 * c + j, at, :] = row.astype(BF16)
        return carry

    lax.fori_loop(0, (CY + 3) * FZ // 32 + 1, build, 0)

    row16 = lax.broadcasted_iota(jnp.int32, (16, 128), 0).astype(F32) - 1.0
    row40 = lax.broadcasted_iota(jnp.int32, (TILE, 128), 0).astype(F32) - 1.0
    slot = lax.broadcasted_iota(jnp.int32, (1, 128), 1)
    blank = jnp.zeros((8, 256), F32)

    def block(b, k):
        at = pl.ds(pl.multiple_of(SLOT * b, SLOT), SLOT)
        t = cell[b]
        brick_y = lax.shift_right_logical(t, 6) & 7
        tile = lax.shift_right_logical(t, 2) & 15
        inner = (t & 3) * 8
        here = offset[:, at]
        wz, sz = spline_pair(here[0:1] - row16)
        wy, sy = spline_pair(here[1:2] - row16)
        wx, sx = spline_pair((here[2:3] + inner.astype(F32)) - row40)
        both = jnp.concatenate([wx, sx], axis=1)
        both_high = both.astype(BF16).astype(F32)
        weights = jnp.concatenate([both_high, both_high, both - both_high, blank], axis=0)
        first = pl.multiple_of(128 * brick_y, 128)
        patch = table[tile, pl.ds(first, 11 * FZ), :]
        weights = weights.astype(BF16)
        turned[k, 0:128] = weights
        turned[k, 128:256] = weights
        turn = pl.multiple_of(128 - 32 * (tile & 3), 32)
        product = dot(patch, turned[k, pl.ds(turn, 128), :])
        base = along = cross = None
        for j in range(11):
            v = product[FZ * j : FZ * (j + 1), :128]
            d = product[FZ * j : FZ * (j + 1), 128:]
            w, s = wy[j : j + 1], sy[j : j + 1]
            base = v * w if base is None else base + v * w
            along = v * s if along is None else along + v * s
            cross = d * w if cross is None else cross + d * w

        def reduce(values):
            return jnp.sum(values, axis=0, keepdims=True)

        live = jnp.where(slot < count[b], 1.0, 0.0)
        slope = live * (-1.0 / 72.0)
        fields[:, at] = jnp.concatenate(
            [
                reduce(base * wz) * (live * (1.0 / 216.0)),
                reduce(base * sz) * slope,
                reduce(along * wz) * slope,
                reduce(cross * wz) * slope,
            ],
            axis=0,
        )

    def copy(i):
        at = pl.ds(pl.multiple_of(STEP * SLOT * i, STEP * SLOT), STEP * SLOT)
        return pltpu.make_async_copy(fields.at[:, at], out.at[:, at], sems.at[i])

    def step(i, carry):
        for k in range(STEP):
            block(STEP * i + k, k)
        copy(i).start()
        return carry

    lax.fori_loop(0, BLOCKS // STEP, step, 0)
    for i in range(BLOCKS // STEP):
        copy(i).wait()


def far_kernel(
    place,
    cell,
    count,
    arrived,
    along_x_in,
    along_y_in,
    along_z_in,
    offset_in,
    near_in,
    out,
    along_x,
    along_y,
    along_z,
    offset,
    fields,
    table,
    turned,
    in_sems,
    sems,
):
    copies = fetch(
        (along_x_in, along_y_in.at[place[1]], along_z_in.at[place[2]], offset_in, near_in),
        (along_x, along_y, along_z, offset, fields),
        in_sems,
    )
    turned[...] = jnp.zeros(turned.shape, BF16)
    lane = lax.broadcasted_iota(jnp.int32, (128, 128), 1) & 31
    top_high, top_low = split(arrived[...].T)
    for copy in copies:
        copy.wait()
    top = dot3(top_high, top_low, along_x[0:512], along_x[512:1024])
    z_weight = jnp.concatenate([along_z[...].astype(F32)] * 8, axis=0)
    weight_high, weight_low = split(along_y[...].astype(F32) * z_weight)
    both = jnp.concatenate([weight_high, weight_low], axis=1)
    for c in range(4):
        source = top[:, 128 * c : 128 * c + 128]
        wide = []
        for m in range(4):
            a, b, e = (
                pltpu.roll(source, (128 + to - 8 * m) % 128, 1) if to != 8 * m else source
                for to in (0, 8, 16)
            )
            wide.append(jnp.where(lane < 8, a, jnp.where(lane < 16, b, e)))
        high, low = split(jnp.concatenate(wide, axis=1))
        values = dot(both, jnp.concatenate([high, high], axis=0)) + dot(weight_high, low)
        for m in range(4):
            for r in range(0, 512, 128):
                piece = values[r : r + 128, 128 * m : 128 * m + 128]
                rounded = piece.astype(BF16).astype(F32)
                keep_low = (lane >= 8) & (lane < 16)
                table[4 * c + m, r : r + 128, :] = jnp.where(
                    keep_low, piece - rounded, rounded
                ).astype(BF16)

    row = lax.broadcasted_iota(jnp.int32, (8, 128), 0)
    row_value = row.astype(F32)
    scales = [jnp.where(row < 5 - high, 0.25, 1.0) for high in range(2)]
    starts = [
        jnp.where(row < 5 - high, row_value - 1.0, row_value + (2.0 if high else -6.0))
        for high in range(2)
    ]
    slot = lax.broadcasted_iota(jnp.int32, (1, 128), 1)
    blank = jnp.zeros((8, 256), F32)

    def weigh(position, high):
        scale = jnp.where(high, scales[1], scales[0])
        value, slope = spline_pair(position * scale - jnp.where(high, starts[1], starts[0]))
        return value, slope * scale

    def reduce(values):
        return jnp.sum(values, axis=0, keepdims=True)

    def block(b, k):
        at = pl.ds(pl.multiple_of(SLOT * b, SLOT), SLOT)
        t = cell[b]
        brick_y = lax.shift_right_logical(t, 6) & 7
        brick_x = t & 63
        here = offset[:, at]
        wz, sz = weigh(here[0:1], place[0] == SLABS - 1)
        wy, sy = weigh(here[1:2], (place[1] == SUBS - 1) & (brick_y == CY // 8 - 1))
        wx, sx = weigh(here[2:3], brick_x == NX // 8 - 1)
        pair = jnp.concatenate([wx, sx], axis=1)
        pair_high = pair.astype(BF16).astype(F32)
        weights = jnp.concatenate([pair_high, pair_high, pair - pair_high, blank], axis=0)
        turned[k, 128:160] = weights.astype(BF16)
        first = pl.multiple_of(64 * brick_y, 64)
        patch = table[lax.shift_right_logical(brick_x, 2), pl.ds(first, 64), :]
        turn = pl.multiple_of(128 - 32 * (brick_x & 3), 32)
        product = dot(patch, turned[k, pl.ds(turn, 128), :])
        base = along = cross = None
        for j in range(8):
            v = product[8 * j : 8 * j + 8, :128]
            d = product[8 * j : 8 * j + 8, 128:]
            w, s = wy[j : j + 1], sy[j : j + 1]
            base = v * w if base is None else base + v * w
            along = v * s if along is None else along + v * s
            cross = d * w if cross is None else cross + d * w
        live = jnp.where(slot < count[b], 1.0, 0.0)
        slope = live * (-1.0 / 72.0)
        fields[:, at] = fields[:, at] + jnp.concatenate(
            [
                reduce(base * wz) * (live * (1.0 / 216.0)),
                reduce(base * sz) * slope,
                reduce(along * wz) * slope,
                reduce(cross * wz) * slope,
            ],
            axis=0,
        )

    def copy(i):
        at = pl.ds(pl.multiple_of(STEP * SLOT * i, STEP * SLOT), STEP * SLOT)
        return pltpu.make_async_copy(fields.at[:, at], out.at[:, at], sems.at[i])

    def step(i, carry):
        for k in range(STEP):
            block(STEP * i + k, k)
        copy(i).start()
        return carry

    lax.fori_loop(0, BLOCKS // STEP, step, 0)
    for i in range(BLOCKS // STEP):
        copy(i).wait()


def whole(shape):
    return pl.BlockSpec(shape, lambda i, *_: (0,) * len(shape))


IN_VMEM = pl.BlockSpec(memory_space=pltpu.VMEM)
IN_SMEM = pl.BlockSpec(memory_space=pltpu.SMEM)
ANYWHERE = pl.BlockSpec(memory_space=pl.ANY)


def call(kernel, scalars, near_by, far, out_shape, out_spec, scratch, megabytes, flops, moved):
    return pl.pallas_call(
        kernel,
        in_specs=[IN_SMEM] * len(scalars) + [IN_VMEM] * len(near_by) + [ANYWHERE] * len(far),
        out_specs=out_spec,
        out_shape=jax.ShapeDtypeStruct(out_shape, F32),
        scratch_shapes=scratch,
        compiler_params=pltpu.CompilerParams(vmem_limit_bytes=megabytes * 2**20),
        cost_estimate=pl.CostEstimate(flops=flops, bytes_accessed=moved, transcendentals=0),
    )(*scalars, *near_by, *far)


def on_device(charge_grid, atom_offset, block_cell, block_count):
    consts = CONSTANTS
    p, q = lax.axis_index("slab"), lax.axis_index("sub")
    kind = jnp.where(p == 0, 0, jnp.where(p == SLABS - 1, 2, 1))
    place = jnp.stack([p, q, kind, kind * SUBS + q]).astype(jnp.int32)

    up = [(i, i + 1) for i in range(SLABS - 1)]
    down = [(b, a) for a, b in up]
    up_sub = [(i, i + 1) for i in range(SUBS - 1)]
    down_sub = [(b, a) for a, b in up_sub]

    below = lax.ppermute(charge_grid, "slab", up)
    above = lax.ppermute(charge_grid, "slab", down)
    partial = pl.pallas_call(
        restrict_kernel,
        grid_spec=pltpu.PrefetchScalarGridSpec(
            num_scalar_prefetch=1,
            grid=(1,),
            in_specs=[
                whole((CZ, CY, NX)),
                whole((NX, 128)),
                pl.BlockSpec((1, CZ * CY, 128), lambda i, place: (place[3], 0, 0)),
            ],
            out_specs=whole((512, 128)),
        ),
        out_shape=jax.ShapeDtypeStruct((512, 128), F32),
        compiler_params=pltpu.CompilerParams(vmem_limit_bytes=60 * 2**20),
        cost_estimate=pl.CostEstimate(flops=10**8, bytes_accessed=10**6, transcendentals=0),
    )(place, charge_grid, consts["restrict_x"], consts["restrict_zy"])
    pencil = lax.all_to_all(partial, ("slab", "sub"), 0, 0, tiled=True)

    planes = (below[CZ - 3 :], charge_grid, above[:4])
    left = jnp.concatenate([plane[:, CY - 4 :] for plane in planes], axis=0)
    right = jnp.concatenate([plane[:, :4] for plane in planes], axis=0)
    left = lax.ppermute(left, "sub", up_sub)
    right = lax.ppermute(right, "sub", down_sub)
    near = call(
        near_kernel,
        [place],
        [],
        [charge_grid, below, above, left, right, consts["near_x"]],
        (FY * FZ, FX),
        ANYWHERE,
        [
            pltpu.VMEM((CZ, CY, NX), F32),
            pltpu.VMEM((3, CY, NX), F32),
            pltpu.VMEM((4, CY, NX), F32),
            pltpu.VMEM((15, 4, NX), F32),
            pltpu.VMEM((15, 4, NX), F32),
            pltpu.VMEM((2 * NX, FX), BF16),
            pltpu.VMEM((CY + 24, NX), F32),
            pltpu.VMEM((NX // 128, FY * FZ, 128), F32),
            pltpu.VMEM((FY * FZ, FX), F32),
            pltpu.SemaphoreType.DMA((6,)),
            pltpu.SemaphoreType.DMA((FY * FZ // ROWS,)),
        ],
        60,
        2 * 10**9,
        16 * 10**6,
    )
    pencil, near = lax.optimization_barrier((pencil, near))

    folded = call(
        middle_kernel,
        [place],
        [pencil, *consts["span_y"], *consts["span_z"]],
        [],
        (512, 128),
        IN_VMEM,
        [],
        12,
        2 * 10**8,
        2 * 10**6,
    )
    arrived = lax.all_to_all(folded, "slab", 0, 0, tiled=True)
    near, _ = lax.optimization_barrier((near, folded))
    fields = call(
        atoms_kernel,
        [block_cell, block_count],
        [],
        [near, atom_offset],
        (4, BLOCKS * SLOT),
        ANYWHERE,
        [
            pltpu.VMEM((FY * FZ, FX), F32),
            pltpu.VMEM((3, BLOCKS * SLOT), F32),
            pltpu.VMEM((TILES, FY * FZ, 128), BF16),
            pltpu.VMEM((STEP, 256, 256), BF16),
            pltpu.VMEM((4, BLOCKS * SLOT), F32),
            pltpu.SemaphoreType.DMA((2,)),
            pltpu.SemaphoreType.DMA((BLOCKS // STEP,)),
        ],
        60,
        10**10,
        8 * 10**6,
    )
    return call(
        far_kernel,
        [place, block_cell, block_count],
        [arrived],
        [consts["far_x"], consts["far_y"], consts["far_z"], atom_offset, fields],
        (4, BLOCKS * SLOT),
        ANYWHERE,
        [
            pltpu.VMEM((1024, NX), BF16),
            pltpu.VMEM((512, 128), BF16),
            pltpu.VMEM((64, 128), BF16),
            pltpu.VMEM((3, BLOCKS * SLOT), F32),
            pltpu.VMEM((4, BLOCKS * SLOT), F32),
            pltpu.VMEM((TILES, 512, 128), BF16),
            pltpu.VMEM((STEP, 256, 256), BF16),
            pltpu.SemaphoreType.DMA((5,)),
            pltpu.SemaphoreType.DMA((BLOCKS // STEP,)),
        ],
        60,
        10**9,
        8 * 10**6,
    )


def solution(mesh):
    placed = (
        P("slab", "sub", None),
        P(None, ("slab", "sub")),
        P(("slab", "sub")),
        P(("slab", "sub")),
    )
    return jax.shard_map(
        on_device, mesh=mesh, in_specs=placed, out_specs=P(None, ("slab", "sub")), check_vma=False
    )
```

```python
import math

import jax
import jax.numpy as jnp
import ml_dtypes
import numpy as np
from jax import lax
from jax.experimental import pallas as pl
from jax.experimental.pallas import tpu as pltpu
from jax.sharding import PartitionSpec as P

TAPS = (0.125, 0.5, 0.75, 0.5, 0.125)
SPANS = (2.0, 8.0, 32.0)
NEAR = [math.exp(-0.5 * d * d) for d in range(3)]
NEAR_WEIGHT = 0.5

SLABS, SUBS = 64, 4
CZ, CY, NX = 8, 64, 512
NZ, NY = CZ * SLABS, CY * SUBS
BLOCKS, SLOT = 128, 128

FZ, FY, FX = 16, 72, 640
TZ, TY, TYS = 5, 19, 24
GS = 21
TILE = 40
TILES = 16
ROWS = 384
STEP = 8
PIECES = 8

F32, BF16 = jnp.float32, jnp.bfloat16


def restriction(n):
    matrix = np.zeros((n // 2, n))
    for target in range(n // 2):
        for offset in range(-2, 3):
            if 0 <= 2 * target + offset < n:
                matrix[target, 2 * target + offset] = TAPS[offset + 2]
    return matrix


def restriction_twice(n):
    return restriction(n // 2) @ restriction(n)


def gauss(n, span):
    index = np.arange(n, dtype=np.float64)
    return np.exp(-(((index[:, None] - index[None, :]) / span) ** 2))


def window(matrix, row0, rows, col0, cols):
    out = np.zeros((rows, cols))
    for r in range(rows):
        for c in range(cols):
            if 0 <= row0 + r < matrix.shape[0] and 0 <= col0 + c < matrix.shape[1]:
                out[r, c] = matrix[row0 + r, col0 + c]
    return out


def halves(matrix):
    whole = np.asarray(matrix, np.float32)
    high = whole.astype(ml_dtypes.bfloat16)
    low = (whole - high.astype(np.float32)).astype(ml_dtypes.bfloat16)
    return high, low


def split(values):
    high = values.astype(BF16)
    return high, (values - high.astype(F32)).astype(BF16)


def dot(left, right):
    return jnp.dot(left, right, preferred_element_type=F32)


def dot3(left_high, left_low, right_high, right_low):
    return dot(left_high, right_high) + (dot(left_low, right_high) + dot(left_high, right_low))


SLAB_KINDS = (0, 1, SLABS - 1)


def make_constants():
    rz, ry, rx = restriction_twice(NZ), restriction_twice(NY), restriction_twice(NX)
    restrict_x = np.concatenate([rx[0::2], rx[1::2]]).T.astype(ml_dtypes.bfloat16)
    restrict_zy = np.zeros((3, SUBS, CZ, CY, 128))
    for kind, p in enumerate(SLAB_KINDS):
        mz = window(rz, 2 * p - 1, TZ, CZ * p, CZ)
        for q in range(SUBS):
            my = window(ry, 16 * q - 1, TY, CY * q, CY)
            for zt in range(TZ):
                restrict_zy[kind, q, :, :, zt * TYS : zt * TYS + TY] = (
                    mz[zt][:, None, None] * my.T[None, :, :]
                )
    restrict_zy = restrict_zy.reshape(3 * SUBS, CZ * CY, 128).astype(np.float32)

    span_y = np.zeros((SUBS, 128, 3 * 128))
    span_z = np.zeros((TZ, SLABS, 3, 2, SLABS))
    fine_x = np.zeros((SLABS, 8, FX))
    for s, span in enumerate(SPANS):
        gy, gz, gx = gauss(NY // 4, span), gauss(NZ // 4, span), gauss(NX // 4, span)
        for q in range(SUBS):
            part = window(gy, 16 * q - 1, TY, 0, NY // 4).T
            for x in range(2):
                col = s * 128 + (s * 2 + x) * GS
                span_y[q, x * 64 : x * 64 + 64, col : col + TY] = part
        wide = np.zeros((NZ // 4 + 8, NZ // 4))
        wide[1 : 1 + NZ // 4] = gz * span ** (-1.5)
        for k in range(TZ):
            rows = wide[k : k + NZ // 4 : 2]
            span_z[k, :, s] = rows.reshape(SLABS, SLABS, 2).transpose(0, 2, 1)
        px = rx.T @ gx
        for x in range(2):
            fine_x[:, s * 2 + x, 1 : 1 + NX] = px[:, x::2].T
    span_z = span_z.reshape(TZ * SLABS, 3 * 128)
    fine_x = fine_x.reshape(SLABS * 8, FX)

    prolong_y = np.zeros((SUBS, FY, FZ, 128))
    for q in range(SUBS):
        part = window(ry.T, CY * q - 1, CY + 3, 16 * q - 1, TY)
        for zo in range(TZ):
            prolong_y[q, : CY + 3, :, zo * TYS : zo * TYS + TY] = part[:, None, :]
    prolong_y = prolong_y.reshape(SUBS, FY * FZ, 128).astype(ml_dtypes.bfloat16)
    prolong_z = np.zeros((3, 8, FZ, 128))
    for kind, p in enumerate(SLAB_KINDS):
        part = window(rz.T, CZ * p - 1, CZ + 3, 2 * p - 1, TZ)
        for zo in range(TZ):
            prolong_z[kind, :, : CZ + 3, zo * TYS : zo * TYS + TY] = part[None, :, zo, None]
    prolong_z = prolong_z.reshape(3, 8 * FZ, 128).astype(ml_dtypes.bfloat16)
    near_x = np.zeros((NX, FX))
    for node in range(NX):
        for offset in range(-2, 3):
            if 0 <= node + offset < NX:
                near_x[node + offset, node + 1] = NEAR_WEIGHT * NEAR[abs(offset)]
    return dict(
        near_x=np.concatenate(halves(near_x)),
        restrict_x=restrict_x,
        restrict_zy=restrict_zy,
        span_y=halves(span_y),
        span_z=halves(span_z),
        fine_x=np.concatenate(halves(fine_x)),
        prolong_y=prolong_y,
        prolong_z=prolong_z,
    )


CONSTANTS = make_constants()


def restrict_kernel(place, charge, along_x, along_zy, out):
    values = charge[...].reshape(CZ * CY, NX)
    high, low = split(values)
    narrow = dot(high, along_x[...]) + dot(low, along_x[...])
    narrow_high, narrow_low = split(narrow.T)
    zy_high, zy_low = split(along_zy[0])
    partial = dot3(narrow_high, narrow_low, zy_high, zy_low)
    for x in range(2):
        for q in range(SUBS):
            out[pl.ds(2 * q + x, SLABS, stride=8), :] = partial[x * SLABS : (x + 1) * SLABS]


def middle_kernel(place, pencil, y_high, y_low, z_high, z_low, out):
    q = place[1]
    lane = lax.broadcasted_iota(jnp.int32, (SLABS, 128), 1)
    gathered = [None] * TZ
    for source in range(SUBS):
        for x in range(2):
            rows = pencil[pl.ds(2 * source + x, SLABS, stride=8), :]
            first = 64 * x - 1 + 16 * source
            inside = (lane >= first) & (lane < first + TY)
            for zt in range(TZ):
                shift = (first + 256 - TYS * zt) % 128
                term = jnp.where(inside, pltpu.roll(rows, shift, 1), 0.0)
                gathered[zt] = term if gathered[zt] is None else gathered[zt] + term
    even = gathered[1] + pltpu.roll(gathered[3], 1, 0)
    odd = gathered[2] + pltpu.roll(gathered[4], 1, 0) + pltpu.roll(gathered[0], SLABS - 1, 0)
    top_high, top_low = split(jnp.concatenate([even, odd], axis=0))
    mixed = dot3(top_high, top_low, y_high[q], y_low[q])
    stacked = jnp.concatenate([mixed[:, :128], mixed[:, 128:256], mixed[:, 256:]], axis=0)
    stacked_high, stacked_low = split(stacked)
    folded = dot3(z_high[...], z_low[...], stacked_high, stacked_low)
    for g in range(6):
        total = None
        for k in range(TZ):
            piece = folded[k * SLABS : (k + 1) * SLABS]
            moved = pltpu.roll(piece, (256 + TYS * k - GS * g) % 128, 1)
            term = jnp.where((lane >= TYS * k) & (lane < TYS * k + TY), moved, 0.0)
            total = term if total is None else total + term
        out[pl.ds(g, SLABS, stride=8), :] = total
    for g in range(6, 8):
        out[pl.ds(g, SLABS, stride=8), :] = jnp.zeros((SLABS, 128), F32)


def fetch(sources, targets, sems):
    copies = [
        pltpu.make_async_copy(source, target, sems.at[i])
        for i, (source, target) in enumerate(zip(sources, targets))
    ]
    for copy in copies:
        copy.start()
    return copies


def near_kernel(
    place,
    charge_in,
    z_low_in,
    z_high_in,
    y_low_in,
    y_high_in,
    along_x_in,
    out,
    charge,
    z_low,
    z_high,
    y_low,
    y_high,
    along_x,
    rows,
    wide,
    grid,
    sems,
    out_sems,
):
    copies = fetch(
        (charge_in, z_low_in, z_high_in, y_low_in, y_high_in, along_x_in),
        (charge, z_low, z_high, y_low, y_high, along_x),
        sems,
    )
    for copy in copies[:5]:
        copy.wait()
    p, q = place[0], place[1]

    def stencil(at):
        return NEAR[2] * (at(0) + at(4)) + (NEAR[1] * (at(1) + at(3)) + at(2))

    def plane(k):
        if k < 3:
            return z_low[k]
        return charge[k - 3] if k < 3 + CZ else z_high[k - 3 - CZ]

    node = lax.broadcasted_iota(jnp.int32, (FY, 128), 0) + (CY * q - 1)
    keep_y = jnp.where((node >= 0) & (node < NY), 1.0, 0.0)
    keep_y = jnp.concatenate([keep_y] * (NX // 128), axis=1)
    for zo in range(CZ + 3):
        rows[8 : 8 + CY] = stencil(lambda d: plane(zo + d))
        rows[4:8] = stencil(lambda d: y_low[zo + d])
        rows[8 + CY : 12 + CY] = stencil(lambda d: y_high[zo + d])
        rows[12 + CY : 24 + CY] = jnp.zeros((12, NX), F32)
        total = stencil(lambda d: rows[5 + d : 5 + d + FY]) * keep_y
        if zo == 0:
            total = total * jnp.where(p > 0, 1.0, 0.0)
        elif zo >= 1 + CZ:
            total = total * jnp.where(p < SLABS - 1, 1.0, 0.0)
        for piece in range(NX // 128):
            at = 128 * piece
            wide[piece, pl.ds(zo, FY, stride=FZ), :] = total[:, at : at + 128]
    for zo in range(CZ + 3, FZ):
        for piece in range(NX // 128):
            wide[piece, pl.ds(zo, FY, stride=FZ), :] = jnp.zeros((FY, 128), F32)

    copies[5].wait()
    stores = []
    for i in range(FY * FZ // ROWS):
        at = pl.ds(ROWS * i, ROWS)
        values = jnp.concatenate([wide[c, at, :] for c in range(NX // 128)], axis=1)
        high, low = split(values)
        for k0, k1, n0, n1 in ((0, 384, 0, 256), (128, 512, 256, 512), (384, 512, 512, 640)):
            grid[at, n0:n1] = dot3(
                high[:, k0:k1],
                low[:, k0:k1],
                along_x[k0:k1, n0:n1],
                along_x[NX + k0 : NX + k1, n0:n1],
            )
        stores.append(pltpu.make_async_copy(grid.at[at], out.at[at], out_sems.at[i]))
        stores[-1].start()
    for store in stores:
        store.wait()


def spline_pair(distance):
    outer = jnp.maximum(2.0 - jnp.abs(distance), 0.0)
    inner = jnp.maximum(outer - 1.0, 0.0)
    outer_square = outer * outer
    inner_square = 4.0 * (inner * inner)
    value = outer_square * outer - inner_square * inner
    slope = inner_square - outer_square
    return value, jnp.where(distance < 0.0, -slope, slope)


def atoms_kernel(
    place,
    cell,
    count,
    arrived,
    near_in,
    along_x_in,
    along_y_in,
    along_z_in,
    offset_in,
    out,
    near,
    along_x,
    along_y,
    along_z,
    offset,
    table,
    grid,
    turned,
    fields,
    in_sems,
    sems,
):
    chunks = [pl.ds(ROWS * i, ROWS) for i in range(FY * FZ // ROWS)]
    copies = fetch(
        [along_x_in, along_y_in.at[place[1]], along_z_in.at[place[2]]]
        + [near_in.at[at] for at in chunks]
        + [offset_in],
        [along_x, along_y, along_z] + [near.at[at] for at in chunks] + [offset],
        in_sems,
    )
    top_high, top_low = split(arrived[...].T)
    copies[0].wait()
    top = dot3(top_high, top_low, along_x[0:512], along_x[512:1024])
    high, low = split(top)
    twice = jnp.concatenate([high, high], axis=0)
    copies[1].wait()
    copies[2].wait()
    z_weight = jnp.concatenate([along_z[...].astype(F32)] * (ROWS // 128), axis=0)
    lane = lax.broadcasted_iota(jnp.int32, (16, 128), 1)

    def pieces(at):
        values = grid[at, :]
        fine_high = values.astype(BF16).astype(F32)
        fine_low = values - fine_high
        h = [fine_high[:, 128 * c : 128 * c + 128] for c in range(5)]
        b = [pltpu.roll(fine_low[:, 128 * c : 128 * c + 128], TILE, 1) for c in range(5)]
        e = [pltpu.roll(h[c], 2 * TILE, 1) for c in range(5)]
        for c in range(4):
            for j in range(4):
                one, two, three = h[c], b[c], e[c]
                if j == 3:
                    one = jnp.where(lane < 64, h[c + 1], one)
                    two = jnp.where(lane >= TILE, b[c + 1], two)
                    three = jnp.where(lane >= 2 * TILE, e[c + 1], three)
                place_in = (lane + (128 - 32 * j)) & 127
                row = jnp.where(place_in < TILE, one, jnp.where(place_in < 2 * TILE, two, three))
                table[4 * c + j, at, :] = row.astype(BF16)

    def build(i, carry):
        for k in range(PIECES):
            pieces(pl.ds(pl.multiple_of(16 * (PIECES * i + k), 16), 16))
        return carry

    for i, at in enumerate(chunks):
        weight_high, weight_low = split(along_y[at, :].astype(F32) * z_weight)
        both = jnp.concatenate([weight_high, weight_low], axis=1)
        far = dot(both, twice) + dot(weight_high, low)
        copies[3 + i].wait()
        grid[at, :] = near[at, :] + far
        per = ROWS // (16 * PIECES)
        lax.fori_loop(per * i, per * (i + 1), build, 0)
    copies[-1].wait()

    row16 = lax.broadcasted_iota(jnp.int32, (16, 128), 0).astype(F32) - 1.0
    row40 = lax.broadcasted_iota(jnp.int32, (TILE, 128), 0).astype(F32) - 1.0
    slot = lax.broadcasted_iota(jnp.int32, (1, 128), 1)
    blank = jnp.zeros((8, 256), F32)

    def block(b, k):
        at = pl.ds(pl.multiple_of(SLOT * b, SLOT), SLOT)
        t = cell[b]
        brick_y = lax.shift_right_logical(t, 6) & 7
        tile = lax.shift_right_logical(t, 2) & 15
        inner = (t & 3) * 8
        here = offset[:, at]
        wz, sz = spline_pair(here[0:1] - row16)
        wy, sy = spline_pair(here[1:2] - row16)
        wx, sx = spline_pair((here[2:3] + inner.astype(F32)) - row40)
        both = jnp.concatenate([wx, sx], axis=1)
        both_high = both.astype(BF16).astype(F32)
        weights = jnp.concatenate([both_high, both_high, both - both_high, blank], axis=0)
        first = pl.multiple_of(128 * brick_y, 128)
        patch = table[tile, pl.ds(first, 11 * FZ), :]
        weights = weights.astype(BF16)
        for i in range(4):
            turn = pl.multiple_of(32 * ((tile + i) & 3), 32)
            turned[k, pl.ds(turn, 32), :] = weights[32 * i : 32 * i + 32]
        product = dot(patch, turned[k])
        base = along = cross = None
        for j in range(11):
            v = product[FZ * j : FZ * (j + 1), :128]
            d = product[FZ * j : FZ * (j + 1), 128:]
            w, s = wy[j : j + 1], sy[j : j + 1]
            base = v * w if base is None else base + v * w
            along = v * s if along is None else along + v * s
            cross = d * w if cross is None else cross + d * w

        def reduce(values):
            return jnp.sum(values, axis=0, keepdims=True)

        live = jnp.where(slot < count[b], 1.0, 0.0)
        slope = live * (-1.0 / 72.0)
        fields[:, at] = jnp.concatenate(
            [
                reduce(base * wz) * (live * (1.0 / 216.0)),
                reduce(base * sz) * slope,
                reduce(along * wz) * slope,
                reduce(cross * wz) * slope,
            ],
            axis=0,
        )

    def copy(i):
        at = pl.ds(pl.multiple_of(STEP * SLOT * i, STEP * SLOT), STEP * SLOT)
        return pltpu.make_async_copy(fields.at[:, at], out.at[:, at], sems.at[i])

    def step(i, carry):
        for k in range(STEP):
            block(STEP * i + k, k)
        copy(i).start()
        return carry

    lax.fori_loop(0, BLOCKS // STEP, step, 0)
    for i in range(BLOCKS // STEP):
        copy(i).wait()


def whole(shape):
    return pl.BlockSpec(shape, lambda i, *_: (0,) * len(shape))


IN_VMEM = pl.BlockSpec(memory_space=pltpu.VMEM)
IN_SMEM = pl.BlockSpec(memory_space=pltpu.SMEM)
ANYWHERE = pl.BlockSpec(memory_space=pl.ANY)


def call(kernel, scalars, near_by, far, out_shape, out_spec, scratch, megabytes, flops, moved):
    return pl.pallas_call(
        kernel,
        in_specs=[IN_SMEM] * len(scalars) + [IN_VMEM] * len(near_by) + [ANYWHERE] * len(far),
        out_specs=out_spec,
        out_shape=jax.ShapeDtypeStruct(out_shape, F32),
        scratch_shapes=scratch,
        compiler_params=pltpu.CompilerParams(vmem_limit_bytes=megabytes * 2**20),
        cost_estimate=pl.CostEstimate(flops=flops, bytes_accessed=moved, transcendentals=0),
    )(*scalars, *near_by, *far)


def on_device(charge_grid, atom_offset, block_cell, block_count):
    consts = CONSTANTS
    p, q = lax.axis_index("slab"), lax.axis_index("sub")
    kind = jnp.where(p == 0, 0, jnp.where(p == SLABS - 1, 2, 1))
    place = jnp.stack([p, q, kind, kind * SUBS + q]).astype(jnp.int32)

    up_sub = [(i, i + 1) for i in range(SUBS - 1)]
    down_sub = [(b, a) for a, b in up_sub]

    inner = [(i, i ^ 1) for i in range(SLABS)]
    outer = [(i, i + 1 if i % 2 else i - 1) for i in range(1, SLABS - 1)]
    twin = lax.ppermute(charge_grid, "slab", inner)
    other = lax.ppermute(charge_grid, "slab", outer)
    partial = pl.pallas_call(
        restrict_kernel,
        grid_spec=pltpu.PrefetchScalarGridSpec(
            num_scalar_prefetch=1,
            grid=(1,),
            in_specs=[
                whole((CZ, CY, NX)),
                whole((NX, 128)),
                pl.BlockSpec((1, CZ * CY, 128), lambda i, place: (place[3], 0, 0)),
            ],
            out_specs=whole((512, 128)),
        ),
        out_shape=jax.ShapeDtypeStruct((512, 128), F32),
        compiler_params=pltpu.CompilerParams(vmem_limit_bytes=60 * 2**20),
        cost_estimate=pl.CostEstimate(flops=10**8, bytes_accessed=10**6, transcendentals=0),
    )(place, charge_grid, consts["restrict_x"], consts["restrict_zy"])
    pencil = lax.all_to_all(partial, ("slab", "sub"), 0, 0, tiled=True)

    odd = p % 2 == 1
    below = jnp.where(odd, twin[CZ - 3 :], other[CZ - 3 :])
    above = jnp.where(odd, other[:4], twin[:4])
    planes = (below, charge_grid, above)
    left = jnp.concatenate([plane[:, CY - 4 :] for plane in planes], axis=0)
    right = jnp.concatenate([plane[:, :4] for plane in planes], axis=0)
    left = lax.ppermute(left, "sub", up_sub)
    right = lax.ppermute(right, "sub", down_sub)
    pencil, left, right = lax.optimization_barrier((pencil, left, right))

    folded = call(
        middle_kernel,
        [place],
        [pencil, *consts["span_y"], *consts["span_z"]],
        [],
        (512, 128),
        IN_VMEM,
        [],
        12,
        2 * 10**8,
        2 * 10**6,
    )
    arrived = lax.all_to_all(folded, "slab", 0, 0, tiled=True)
    left, right, _ = lax.optimization_barrier((left, right, folded))
    near = call(
        near_kernel,
        [place],
        [],
        [charge_grid, below, above, left, right, consts["near_x"]],
        (FY * FZ, FX),
        ANYWHERE,
        [
            pltpu.VMEM((CZ, CY, NX), F32),
            pltpu.VMEM((3, CY, NX), F32),
            pltpu.VMEM((4, CY, NX), F32),
            pltpu.VMEM((15, 4, NX), F32),
            pltpu.VMEM((15, 4, NX), F32),
            pltpu.VMEM((2 * NX, FX), BF16),
            pltpu.VMEM((CY + 24, NX), F32),
            pltpu.VMEM((NX // 128, FY * FZ, 128), F32),
            pltpu.VMEM((FY * FZ, FX), F32),
            pltpu.SemaphoreType.DMA((6,)),
            pltpu.SemaphoreType.DMA((FY * FZ // ROWS,)),
        ],
        60,
        2 * 10**9,
        16 * 10**6,
    )
    return call(
        atoms_kernel,
        [place, block_cell, block_count],
        [arrived],
        [near, consts["fine_x"], consts["prolong_y"], consts["prolong_z"], atom_offset],
        (4, BLOCKS * SLOT),
        ANYWHERE,
        [
            pltpu.VMEM((FY * FZ, FX), F32),
            pltpu.VMEM((1024, FX), BF16),
            pltpu.VMEM((FY * FZ, 128), BF16),
            pltpu.VMEM((128, 128), BF16),
            pltpu.VMEM((3, BLOCKS * SLOT), F32),
            pltpu.VMEM((TILES, FY * FZ, 128), BF16),
            pltpu.VMEM((FY * FZ, FX), F32),
            pltpu.VMEM((STEP, 128, 256), BF16),
            pltpu.VMEM((4, BLOCKS * SLOT), F32),
            pltpu.SemaphoreType.DMA((4 + FY * FZ // ROWS,)),
            pltpu.SemaphoreType.DMA((BLOCKS // STEP,)),
        ],
        60,
        10**9,
        8 * 10**6,
    )


def solution(mesh):
    placed = (
        P("slab", "sub", None),
        P(None, ("slab", "sub")),
        P(("slab", "sub")),
        P(("slab", "sub")),
    )
    return jax.shard_map(
        on_device, mesh=mesh, in_specs=placed, out_specs=P(None, ("slab", "sub")), check_vma=False
    )
```

```python
import math

import jax
import jax.numpy as jnp
import ml_dtypes
import numpy as np
from jax import lax
from jax.experimental import pallas as pl
from jax.experimental.pallas import tpu as pltpu
from jax.sharding import PartitionSpec as P

TAPS = (0.125, 0.5, 0.75, 0.5, 0.125)
SPANS = (2.0, 8.0, 32.0)
NEAR = [math.exp(-0.5 * d * d) for d in range(3)]
NEAR_WEIGHT = 0.5

SLABS, SUBS = 64, 4
CZ, CY, NX = 8, 64, 512
NZ, NY = CZ * SLABS, CY * SUBS
BLOCKS, SLOT = 128, 128

FZ, FY, FX = 16, 72, 640
TZ, TY, TYS = 5, 19, 24
GS = 21
TILE = 40
TILES = 16
ROWS = 384
STEP = 8
PIECES = 24

F32, BF16 = jnp.float32, jnp.bfloat16


def restriction(n):
    matrix = np.zeros((n // 2, n))
    for target in range(n // 2):
        for offset in range(-2, 3):
            if 0 <= 2 * target + offset < n:
                matrix[target, 2 * target + offset] = TAPS[offset + 2]
    return matrix


def restriction_twice(n):
    return restriction(n // 2) @ restriction(n)


def gauss(n, span):
    index = np.arange(n, dtype=np.float64)
    return np.exp(-(((index[:, None] - index[None, :]) / span) ** 2))


def window(matrix, row0, rows, col0, cols):
    out = np.zeros((rows, cols))
    for r in range(rows):
        for c in range(cols):
            if 0 <= row0 + r < matrix.shape[0] and 0 <= col0 + c < matrix.shape[1]:
                out[r, c] = matrix[row0 + r, col0 + c]
    return out


def halves(matrix):
    whole = np.asarray(matrix, np.float32)
    high = whole.astype(ml_dtypes.bfloat16)
    low = (whole - high.astype(np.float32)).astype(ml_dtypes.bfloat16)
    return high, low


def split(values):
    high = values.astype(BF16)
    return high, (values - high.astype(F32)).astype(BF16)


def dot(left, right):
    return jnp.dot(left, right, preferred_element_type=F32)


def dot3(left_high, left_low, right_high, right_low):
    return dot(left_high, right_high) + (dot(left_low, right_high) + dot(left_high, right_low))


SLAB_KINDS = (0, 1, SLABS - 1)


def make_constants():
    rz, ry, rx = restriction_twice(NZ), restriction_twice(NY), restriction_twice(NX)
    restrict_x = np.concatenate([rx[0::2], rx[1::2]]).T.astype(ml_dtypes.bfloat16)
    restrict_zy = np.zeros((3, SUBS, CZ, CY, 128))
    for kind, p in enumerate(SLAB_KINDS):
        mz = window(rz, 2 * p - 1, TZ, CZ * p, CZ)
        for q in range(SUBS):
            my = window(ry, 16 * q - 1, TY, CY * q, CY)
            for zt in range(TZ):
                restrict_zy[kind, q, :, :, zt * TYS : zt * TYS + TY] = (
                    mz[zt][:, None, None] * my.T[None, :, :]
                )
    restrict_zy = restrict_zy.reshape(3 * SUBS, CZ * CY, 128).astype(np.float32)

    span_y = np.zeros((SUBS, 128, 3 * 128))
    span_z = np.zeros((TZ, SLABS, 3, 2, SLABS))
    fine_x = np.zeros((SLABS, 8, FX))
    for s, span in enumerate(SPANS):
        gy, gz, gx = gauss(NY // 4, span), gauss(NZ // 4, span), gauss(NX // 4, span)
        for q in range(SUBS):
            part = window(gy, 16 * q - 1, TY, 0, NY // 4).T
            for x in range(2):
                col = s * 128 + (s * 2 + x) * GS
                span_y[q, x * 64 : x * 64 + 64, col : col + TY] = part
        wide = np.zeros((NZ // 4 + 8, NZ // 4))
        wide[1 : 1 + NZ // 4] = gz * span ** (-1.5)
        for k in range(TZ):
            rows = wide[k : k + NZ // 4 : 2]
            span_z[k, :, s] = rows.reshape(SLABS, SLABS, 2).transpose(0, 2, 1)
        px = rx.T @ gx
        for x in range(2):
            fine_x[:, s * 2 + x, 1 : 1 + NX] = px[:, x::2].T
    span_z = span_z.reshape(TZ * SLABS, 3 * 128)
    fine_x = fine_x.reshape(SLABS * 8, FX)

    prolong_y = np.zeros((SUBS, FY, FZ, 128))
    for q in range(SUBS):
        part = window(ry.T, CY * q - 1, CY + 3, 16 * q - 1, TY)
        for zo in range(TZ):
            prolong_y[q, : CY + 3, :, zo * TYS : zo * TYS + TY] = part[:, None, :]
    prolong_y = prolong_y.reshape(SUBS, FY * FZ, 128).astype(ml_dtypes.bfloat16)
    prolong_z = np.zeros((3, 8, FZ, 128))
    for kind, p in enumerate(SLAB_KINDS):
        part = window(rz.T, CZ * p - 1, CZ + 3, 2 * p - 1, TZ)
        for zo in range(TZ):
            prolong_z[kind, :, : CZ + 3, zo * TYS : zo * TYS + TY] = part[None, :, zo, None]
    prolong_z = prolong_z.reshape(3, 8 * FZ, 128).astype(ml_dtypes.bfloat16)
    near_x = np.zeros((NX, FX))
    for node in range(NX):
        for offset in range(-2, 3):
            if 0 <= node + offset < NX:
                near_x[node + offset, node + 1] = NEAR_WEIGHT * NEAR[abs(offset)]
    return dict(
        near_x=np.concatenate(halves(near_x)),
        restrict_x=restrict_x,
        restrict_zy=restrict_zy,
        span_y=halves(span_y),
        span_z=halves(span_z),
        fine_x=np.concatenate(halves(fine_x)),
        prolong_y=prolong_y,
        prolong_z=prolong_z,
    )


CONSTANTS = make_constants()


def slab_kind(p):
    return jnp.where(p == 0, 0, jnp.where(p == SLABS - 1, 2, 1))


def restrict_kernel(charge_in, along_x_in, along_zy_in, out, charge, along_x, along_zy, sems):
    mine = slab_kind(lax.axis_index("slab")) * SUBS + lax.axis_index("sub")
    half = CZ // 2
    first, second = pl.ds(0, half), pl.ds(half, half)
    copies = fetch(
        (along_x_in, charge_in.at[first], along_zy_in.at[mine], charge_in.at[second]),
        (along_x, charge.at[first], along_zy, charge.at[second]),
        sems,
    )
    copies[0].wait()
    narrow = []
    for part, copy in enumerate((copies[1], copies[3])):
        copy.wait()
        values = charge[half * part : half * (part + 1)].reshape(half * CY, NX)
        high, low = split(values)
        narrow.append((dot(high, along_x[...]) + dot(low, along_x[...])).T)
    copies[2].wait()
    narrow_high, narrow_low = split(jnp.concatenate(narrow, axis=1))
    zy_high, zy_low = split(along_zy[...])
    partial = dot3(narrow_high, narrow_low, zy_high, zy_low)
    for x in range(2):
        for q in range(SUBS):
            out[pl.ds(2 * q + x, SLABS, stride=8), :] = partial[x * SLABS : (x + 1) * SLABS]


def middle_kernel(place, pencil, y_high, y_low, z_high, z_low, out):
    q = place[1]
    lane = lax.broadcasted_iota(jnp.int32, (SLABS, 128), 1)
    gathered = [None] * TZ
    for source in range(SUBS):
        for x in range(2):
            rows = pencil[pl.ds(2 * source + x, SLABS, stride=8), :]
            first = 64 * x - 1 + 16 * source
            inside = (lane >= first) & (lane < first + TY)
            for zt in range(TZ):
                shift = (first + 256 - TYS * zt) % 128
                term = jnp.where(inside, pltpu.roll(rows, shift, 1), 0.0)
                gathered[zt] = term if gathered[zt] is None else gathered[zt] + term
    even = gathered[1] + pltpu.roll(gathered[3], 1, 0)
    odd = gathered[2] + pltpu.roll(gathered[4], 1, 0) + pltpu.roll(gathered[0], SLABS - 1, 0)
    top_high, top_low = split(jnp.concatenate([even, odd], axis=0))
    mixed = dot3(top_high, top_low, y_high[q], y_low[q])
    stacked = jnp.concatenate([mixed[:, :128], mixed[:, 128:256], mixed[:, 256:]], axis=0)
    stacked_high, stacked_low = split(stacked)
    folded = dot3(z_high[...], z_low[...], stacked_high, stacked_low)
    for g in range(6):
        total = None
        for k in range(TZ):
            piece = folded[k * SLABS : (k + 1) * SLABS]
            moved = pltpu.roll(piece, (256 + TYS * k - GS * g) % 128, 1)
            term = jnp.where((lane >= TYS * k) & (lane < TYS * k + TY), moved, 0.0)
            total = term if total is None else total + term
        out[pl.ds(g, SLABS, stride=8), :] = total
    for g in range(6, 8):
        out[pl.ds(g, SLABS, stride=8), :] = jnp.zeros((SLABS, 128), F32)


def fetch(sources, targets, sems):
    copies = [
        pltpu.make_async_copy(source, target, sems.at[i])
        for i, (source, target) in enumerate(zip(sources, targets))
    ]
    for copy in copies:
        copy.start()
    return copies


def near_kernel(
    place,
    charge_in,
    z_low_in,
    z_high_in,
    y_low_in,
    y_high_in,
    along_x_in,
    out,
    charge,
    z_low,
    z_high,
    y_low,
    y_high,
    along_x,
    rows,
    wide,
    grid,
    sems,
    out_sems,
):
    copies = fetch(
        (charge_in, z_low_in, z_high_in, y_low_in, y_high_in, along_x_in),
        (charge, z_low, z_high, y_low, y_high, along_x),
        sems,
    )
    for copy in copies[:5]:
        copy.wait()
    p, q = place[0], place[1]

    def stencil(at):
        return NEAR[2] * (at(0) + at(4)) + (NEAR[1] * (at(1) + at(3)) + at(2))

    def plane(k):
        if k < 3:
            return z_low[k]
        return charge[k - 3] if k < 3 + CZ else z_high[k - 3 - CZ]

    node = lax.broadcasted_iota(jnp.int32, (FY, 128), 0) + (CY * q - 1)
    keep_y = jnp.where((node >= 0) & (node < NY), 1.0, 0.0)
    keep_y = jnp.concatenate([keep_y] * (NX // 128), axis=1)
    for zo in range(CZ + 3):
        rows[8 : 8 + CY] = stencil(lambda d: plane(zo + d))
        rows[4:8] = stencil(lambda d: y_low[zo + d])
        rows[8 + CY : 12 + CY] = stencil(lambda d: y_high[zo + d])
        rows[12 + CY : 24 + CY] = jnp.zeros((12, NX), F32)
        total = stencil(lambda d: rows[5 + d : 5 + d + FY]) * keep_y
        if zo == 0:
            total = total * jnp.where(p > 0, 1.0, 0.0)
        elif zo >= 1 + CZ:
            total = total * jnp.where(p < SLABS - 1, 1.0, 0.0)
        for piece in range(NX // 128):
            at = 128 * piece
            wide[piece, pl.ds(zo, FY, stride=FZ), :] = total[:, at : at + 128]
    for zo in range(CZ + 3, FZ):
        for piece in range(NX // 128):
            wide[piece, pl.ds(zo, FY, stride=FZ), :] = jnp.zeros((FY, 128), F32)

    copies[5].wait()
    stores = []
    for i in range(FY * FZ // ROWS):
        at = pl.ds(ROWS * i, ROWS)
        values = jnp.concatenate([wide[c, at, :] for c in range(NX // 128)], axis=1)
        high, low = split(values)
        for k0, k1, n0, n1 in ((0, 384, 0, 256), (128, 512, 256, 512), (384, 512, 512, 640)):
            grid[at, n0:n1] = dot3(
                high[:, k0:k1],
                low[:, k0:k1],
                along_x[k0:k1, n0:n1],
                along_x[NX + k0 : NX + k1, n0:n1],
            )
        stores.append(pltpu.make_async_copy(grid.at[at], out.at[at], out_sems.at[i]))
        stores[-1].start()
    for store in stores:
        store.wait()


def spline_pair(distance):
    outer = jnp.maximum(2.0 - jnp.abs(distance), 0.0)
    inner = jnp.maximum(outer - 1.0, 0.0)
    outer_square = outer * outer
    inner_square = 4.0 * (inner * inner)
    value = outer_square * outer - inner_square * inner
    slope = inner_square - outer_square
    return value, jnp.where(distance < 0.0, -slope, slope)


def atoms_kernel(
    place,
    cell,
    count,
    arrived,
    near_in,
    along_x_in,
    along_y_in,
    along_z_in,
    offset_in,
    out,
    near,
    along_x,
    along_y,
    along_z,
    offset,
    table,
    grid,
    turned,
    fields,
    in_sems,
    sems,
):
    chunks = [pl.ds(ROWS * i, ROWS) for i in range(FY * FZ // ROWS)]
    copies = fetch(
        [along_x_in, along_y_in.at[place[1]], along_z_in.at[place[2]]]
        + [near_in.at[at] for at in chunks]
        + [offset_in],
        [along_x, along_y, along_z] + [near.at[at] for at in chunks] + [offset],
        in_sems,
    )
    top_high, top_low = split(arrived[...].T)
    copies[0].wait()
    top = dot3(top_high, top_low, along_x[0:512], along_x[512:1024])
    high, low = split(top)
    twice = jnp.concatenate([high, high], axis=0)
    copies[1].wait()
    copies[2].wait()
    z_weight = jnp.concatenate([along_z[...].astype(F32)] * (ROWS // 128), axis=0)
    lane = lax.broadcasted_iota(jnp.int32, (16, 128), 1)

    def pieces(at):
        values = grid[at, :]
        fine_high = values.astype(BF16).astype(F32)
        fine_low = values - fine_high
        h = [fine_high[:, 128 * c : 128 * c + 128] for c in range(5)]
        b = [pltpu.roll(fine_low[:, 128 * c : 128 * c + 128], TILE, 1) for c in range(5)]
        e = [pltpu.roll(h[c], 2 * TILE, 1) for c in range(5)]
        for c in range(4):
            for j in range(4):
                one, two, three = h[c], b[c], e[c]
                if j == 3:
                    one = jnp.where(lane < 64, h[c + 1], one)
                    two = jnp.where(lane >= TILE, b[c + 1], two)
                    three = jnp.where(lane >= 2 * TILE, e[c + 1], three)
                place_in = (lane + (128 - 32 * j)) & 127
                row = jnp.where(place_in < TILE, one, jnp.where(place_in < 2 * TILE, two, three))
                table[4 * c + j, at, :] = row.astype(BF16)

    def build(i, carry):
        for k in range(PIECES):
            pieces(pl.ds(pl.multiple_of(16 * (PIECES * i + k), 16), 16))
        return carry

    for i, at in enumerate(chunks):
        weight_high, weight_low = split(along_y[at, :].astype(F32) * z_weight)
        both = jnp.concatenate([weight_high, weight_low], axis=1)
        far = dot(both, twice) + dot(weight_high, low)
        copies[3 + i].wait()
        grid[at, :] = near[at, :] + far
        per = ROWS // (16 * PIECES)
        lax.fori_loop(per * i, per * (i + 1), build, 0)
    copies[-1].wait()

    row16 = lax.broadcasted_iota(jnp.int32, (16, 128), 0).astype(F32) - 1.0
    row40 = lax.broadcasted_iota(jnp.int32, (TILE, 128), 0).astype(F32) - 1.0
    slot = lax.broadcasted_iota(jnp.int32, (1, 128), 1)
    blank = jnp.zeros((8, 256), F32)

    def block(b, k):
        at = pl.ds(pl.multiple_of(SLOT * b, SLOT), SLOT)
        t = cell[b]
        brick_y = lax.shift_right_logical(t, 6) & 7
        tile = lax.shift_right_logical(t, 2) & 15
        inner = (t & 3) * 8
        here = offset[:, at]
        wz, sz = spline_pair(here[0:1] - row16)
        wy, sy = spline_pair(here[1:2] - row16)
        wx, sx = spline_pair((here[2:3] + inner.astype(F32)) - row40)
        both = jnp.concatenate([wx, sx], axis=1)
        both_high = both.astype(BF16).astype(F32)
        weights = jnp.concatenate([both_high, both_high, both - both_high, blank], axis=0)
        first = pl.multiple_of(128 * brick_y, 128)
        patch = table[tile, pl.ds(first, 11 * FZ), :]
        weights = weights.astype(BF16)
        for i in range(4):
            turn = pl.multiple_of(32 * ((tile + i) & 3), 32)
            turned[k, pl.ds(turn, 32), :] = weights[32 * i : 32 * i + 32]
        product = dot(patch, turned[k])
        base = along = cross = None
        for j in range(11):
            v = product[FZ * j : FZ * (j + 1), :128]
            d = product[FZ * j : FZ * (j + 1), 128:]
            w, s = wy[j : j + 1], sy[j : j + 1]
            base = v * w if base is None else base + v * w
            along = v * s if along is None else along + v * s
            cross = d * w if cross is None else cross + d * w

        def reduce(values):
            return jnp.sum(values, axis=0, keepdims=True)

        live = jnp.where(slot < count[b], 1.0, 0.0)
        slope = live * (-1.0 / 72.0)
        fields[:, at] = jnp.concatenate(
            [
                reduce(base * wz) * (live * (1.0 / 216.0)),
                reduce(base * sz) * slope,
                reduce(along * wz) * slope,
                reduce(cross * wz) * slope,
            ],
            axis=0,
        )

    def copy(i):
        at = pl.ds(pl.multiple_of(STEP * SLOT * i, STEP * SLOT), STEP * SLOT)
        return pltpu.make_async_copy(fields.at[:, at], out.at[:, at], sems.at[i])

    def step(i, carry):
        for k in range(STEP):
            block(STEP * i + k, k)
        copy(i).start()
        return carry

    lax.fori_loop(0, BLOCKS // STEP, step, 0)
    for i in range(BLOCKS // STEP):
        copy(i).wait()


IN_VMEM = pl.BlockSpec(memory_space=pltpu.VMEM)
IN_SMEM = pl.BlockSpec(memory_space=pltpu.SMEM)
ANYWHERE = pl.BlockSpec(memory_space=pl.ANY)


def call(kernel, scalars, near_by, far, out_shape, out_spec, scratch, megabytes, flops, moved):
    return pl.pallas_call(
        kernel,
        in_specs=[IN_SMEM] * len(scalars) + [IN_VMEM] * len(near_by) + [ANYWHERE] * len(far),
        out_specs=out_spec,
        out_shape=jax.ShapeDtypeStruct(out_shape, F32),
        scratch_shapes=scratch,
        compiler_params=pltpu.CompilerParams(vmem_limit_bytes=megabytes * 2**20),
        cost_estimate=pl.CostEstimate(flops=flops, bytes_accessed=moved, transcendentals=0),
    )(*scalars, *near_by, *far)


def on_device(charge_grid, atom_offset, block_cell, block_count):
    consts = CONSTANTS
    p, q = lax.axis_index("slab"), lax.axis_index("sub")
    kind = slab_kind(p)
    place = jnp.stack([p, q, kind, kind * SUBS + q]).astype(jnp.int32)

    up_sub = [(i, i + 1) for i in range(SUBS - 1)]
    down_sub = [(b, a) for a, b in up_sub]

    inner = [(i, i ^ 1) for i in range(SLABS)]
    outer = [(i, i + 1 if i % 2 else i - 1) for i in range(1, SLABS - 1)]
    twin = lax.ppermute(charge_grid, "slab", inner)
    other = lax.ppermute(charge_grid, "slab", outer)
    partial = call(
        restrict_kernel,
        [],
        [],
        [charge_grid, consts["restrict_x"], consts["restrict_zy"]],
        (512, 128),
        IN_VMEM,
        [
            pltpu.VMEM((CZ, CY, NX), F32),
            pltpu.VMEM((NX, 128), BF16),
            pltpu.VMEM((CZ * CY, 128), F32),
            pltpu.SemaphoreType.DMA((4,)),
        ],
        60,
        10**8,
        10**6,
    )
    pencil = lax.all_to_all(partial, ("slab", "sub"), 0, 0, tiled=True)

    odd = p % 2 == 1
    below = jnp.where(odd, twin[CZ - 3 :], other[CZ - 3 :])
    above = jnp.where(odd, other[:4], twin[:4])
    planes = (below, charge_grid, above)
    left = jnp.concatenate([plane[:, CY - 4 :] for plane in planes], axis=0)
    right = jnp.concatenate([plane[:, :4] for plane in planes], axis=0)
    left = lax.ppermute(left, "sub", up_sub)
    right = lax.ppermute(right, "sub", down_sub)
    pencil, left, right = lax.optimization_barrier((pencil, left, right))

    folded = call(
        middle_kernel,
        [place],
        [pencil, *consts["span_y"], *consts["span_z"]],
        [],
        (512, 128),
        IN_VMEM,
        [],
        12,
        2 * 10**8,
        2 * 10**6,
    )
    arrived = lax.all_to_all(folded, "slab", 0, 0, tiled=True)
    left, right, _ = lax.optimization_barrier((left, right, folded))
    near = call(
        near_kernel,
        [place],
        [],
        [charge_grid, below, above, left, right, consts["near_x"]],
        (FY * FZ, FX),
        ANYWHERE,
        [
            pltpu.VMEM((CZ, CY, NX), F32),
            pltpu.VMEM((3, CY, NX), F32),
            pltpu.VMEM((4, CY, NX), F32),
            pltpu.VMEM((15, 4, NX), F32),
            pltpu.VMEM((15, 4, NX), F32),
            pltpu.VMEM((2 * NX, FX), BF16),
            pltpu.VMEM((CY + 24, NX), F32),
            pltpu.VMEM((NX // 128, FY * FZ, 128), F32),
            pltpu.VMEM((FY * FZ, FX), F32),
            pltpu.SemaphoreType.DMA((6,)),
            pltpu.SemaphoreType.DMA((FY * FZ // ROWS,)),
        ],
        60,
        2 * 10**9,
        16 * 10**6,
    )
    return call(
        atoms_kernel,
        [place, block_cell, block_count],
        [arrived],
        [near, consts["fine_x"], consts["prolong_y"], consts["prolong_z"], atom_offset],
        (4, BLOCKS * SLOT),
        ANYWHERE,
        [
            pltpu.VMEM((FY * FZ, FX), F32),
            pltpu.VMEM((1024, FX), BF16),
            pltpu.VMEM((FY * FZ, 128), BF16),
            pltpu.VMEM((128, 128), BF16),
            pltpu.VMEM((3, BLOCKS * SLOT), F32),
            pltpu.VMEM((TILES, FY * FZ, 128), BF16),
            pltpu.VMEM((FY * FZ, FX), F32),
            pltpu.VMEM((STEP, 128, 256), BF16),
            pltpu.VMEM((4, BLOCKS * SLOT), F32),
            pltpu.SemaphoreType.DMA((4 + FY * FZ // ROWS,)),
            pltpu.SemaphoreType.DMA((BLOCKS // STEP,)),
        ],
        60,
        10**9,
        8 * 10**6,
    )


def solution(mesh):
    placed = (
        P("slab", "sub", None),
        P(None, ("slab", "sub")),
        P(("slab", "sub")),
        P(("slab", "sub")),
    )
    return jax.shard_map(
        on_device, mesh=mesh, in_specs=placed, out_specs=P(None, ("slab", "sub")), check_vma=False
    )
```
